128 devices in a mesh: grp: 8 (over z, core), dev: 16 (over x, y).
Axes of the slice: x: 4, y: 4, z: 4, core: 2. Of those that a mesh axis runs over, the one named last changes fastest.
Arguments:
- src_leaf: bfloat16 [8192, 64, 32], P(('grp', 'dev')), may hold values from -6 to 6
- adj_leaf: bfloat16 [8192, 64, 32], P(('grp', 'dev')), may hold values from -6 to 6
- up_leaf: bfloat16 [8192, 64, 64], P(('grp', 'dev')), may hold values from -0.5 to 0.5
- up_mid: bfloat16 [1024, 64, 64], P(('grp', 'dev')), may hold values from -0.5 to 0.5
- couple_leaf: bfloat16 [8192, 16, 64, 64], P(('grp', 'dev')), may hold values from -0.1875 to 0.1875
- couple_mid: bfloat16 [1024, 16, 64, 64], P(('grp', 'dev')), may hold values from -0.1875 to 0.1875
- couple_top: bfloat16 [128, 16, 64, 64], P(('grp', 'dev')), may hold values from -0.1875 to 0.1875
- send_slots: int32 [128, 128, 3], P(('grp', 'dev')), may hold values from 0 to 71, as said below
- leaf_list: int32 [8192, 16], P(('grp', 'dev')), may hold values from 0 to 382, as said below
- mid_list: int32 [1024, 16], P(('grp', 'dev')), may hold values from 2 to 383, as said below
- top_list: int32 [128, 16], P(('grp', 'dev')), may hold values from 0 to 127, as said below
Outputs:
- leaf_forward: bfloat16 [8192, 64, 32], P(('grp', 'dev'))
- leaf_adjoint: bfloat16 [8192, 64, 32], P(('grp', 'dev'))
The draws below stay inside these ranges and needn't reach their ends.
Inputs may be any that keep to these rules, and one draw needn't show every extreme that they name: `send_slots`: slots s < 2 of each sender and receiver name distinct leaves of the sender's pool; the other slots name second-level clusters. `leaf_list`: every entry is p * 3 + s with s < 2; every such slot is named by some leaf of each device. `mid_list`: every entry is p * 3 + s with s >= 2; every such slot is named by some cluster of each device. `top_list`: column 0 names every top-level cluster once.
All inputs are finite; a program needn't handle non-finite values.
Results may differ from the reference program's by a relative error of at most 0.009.
Values may be sent and summed in bfloat16 or wider, within the bound.
No kernel may reach another device: no remote copies, remote signals or barrier semaphores. Data moves between devices by JAX's collectives and lax.ppermute only.
A program may use at most 192 MiB of HBM per device.

```python
import jax
import jax.numpy as jnp
from jax import lax

R = 64
NF = 32
NA = 32
K3 = 16
K2 = 16
K1 = 16
CAP3 = 2
CAP2 = 1
CAP = 3
PEERS = 128
LEAF_DEV = 64
MID_DEV = 8
POOL = 72
NC3 = 8192
NC2 = 1024
NC1 = 128


def spread_slots(seed_key, row_count, column_count, first_slot, slot_count):
    entry_count = row_count * column_count
    cover_count = PEERS * slot_count
    key_list = jax.random.split(seed_key, 3)
    covering = jax.random.permutation(key_list[0], cover_count)
    remaining = jax.random.randint(key_list[1], (entry_count - cover_count,), 0, cover_count)
    slot_ids = jax.random.permutation(key_list[2], jnp.concatenate([covering, remaining]))
    placed = slot_ids // slot_count * CAP + first_slot + slot_ids % slot_count
    return placed.reshape(row_count, column_count)


def draw_send_slots(key, part):
    key = jax.random.fold_in(key, 11)
    leaf_key, mid_key = jax.random.split(key)
    pair_keys = jax.random.split(leaf_key, PEERS * PEERS)
    chosen = jax.vmap(lambda subkey: jax.random.permutation(subkey, LEAF_DEV)[:CAP3])(pair_keys)
    chosen = chosen.reshape(PEERS, PEERS, CAP3)
    mid_picks = LEAF_DEV + jax.random.randint(mid_key, (PEERS, PEERS, CAP2), 0, MID_DEV)
    return jnp.concatenate([chosen, mid_picks], axis=2).astype(jnp.int32)


def draw_leaf_list(key, part):
    key = jax.random.fold_in(key, 23)
    device_keys = jax.random.split(key, PEERS)
    lists = jax.vmap(lambda subkey: spread_slots(subkey, LEAF_DEV, K3, 0, CAP3))(device_keys)
    return lists.reshape(PEERS * LEAF_DEV, K3).astype(jnp.int32)


def draw_mid_list(key, part):
    key = jax.random.fold_in(key, 31)
    device_keys = jax.random.split(key, PEERS)
    lists = jax.vmap(lambda subkey: spread_slots(subkey, MID_DEV, K2, CAP3, CAP2))(device_keys)
    return lists.reshape(PEERS * MID_DEV, K2).astype(jnp.int32)


def draw_top_list(key, part):
    key = jax.random.fold_in(key, 37)
    head_key, tail_key = jax.random.split(key)
    leading = jax.random.permutation(head_key, NC1)
    trailing = jax.random.randint(tail_key, (NC1, K1 - 1), 0, NC1)
    return jnp.concatenate([leading[:, None], trailing], axis=1).astype(jnp.int32)


def block_scale(own_key, dims, shards, low, largest):
    loudness = 1.0
    for position, parts in shards:
        draws = jax.random.uniform(jax.random.fold_in(jax.random.fold_in(own_key, 6), position), (parts,), jnp.float32, low / len(shards), largest / len(shards))
        loudness = loudness * jnp.repeat(jnp.exp(draws), dims[position] // parts).reshape((-1,) + (1,) * (len(dims) - 1 - position))
    return loudness


def centred(own_key, extent, deviation, reach, pieces=(), kind=jnp.bfloat16):
    values = deviation * jax.random.normal(own_key, extent, jnp.float32)
    if pieces:
        values = values * block_scale(own_key, extent, pieces, -0.22, 0.18)
    return jnp.clip(values, -reach, reach).astype(kind)


def setup_inputs(seed: int = 0) -> dict:
    key_of = jax.random.split(jax.random.key(seed), 12)
    return {
        "src_leaf": centred(key_of[0], (NC3, R, NF), 1.0, 6.0, ((0, 128),)),
        "adj_leaf": centred(key_of[1], (NC3, R, NA), 1.0, 6.0, ((0, 128),)),
        "up_leaf": centred(key_of[2], (NC3, R, R), (2 * R) ** -0.5, 0.5, ((0, 128),)),
        "up_mid": centred(key_of[3], (NC2, R, R), (2 * R) ** -0.5, 0.5, ((0, 128),)),
        "couple_leaf": centred(key_of[4], (NC3, K3, R, R), (K3 * R) ** -0.5, 0.1875, ((0, 128),)),
        "couple_mid": centred(key_of[5], (NC2, K2, R, R), (K2 * R) ** -0.5, 0.1875, ((0, 128),)),
        "couple_top": centred(key_of[6], (NC1, K1, R, R), (K1 * R) ** -0.5, 0.1875, ((0, 128),)),
        "send_slots": draw_send_slots(jax.random.fold_in(key_of[11], 71), 0),
        "leaf_list": draw_leaf_list(jax.random.fold_in(key_of[11], 71), 0),
        "mid_list": draw_mid_list(jax.random.fold_in(key_of[11], 71), 0),
        "top_list": draw_top_list(jax.random.fold_in(key_of[11], 71), 0),
    }


HIGH = lax.Precision.HIGHEST


def lift_level(transfer, coeffs):
    parents = transfer.shape[0] // 8
    basis_size = transfer.shape[1]
    return jnp.einsum("cirk,cirf->ckf", transfer.reshape(parents, 8, basis_size, basis_size).astype(jnp.float32), coeffs.reshape(parents, 8, basis_size, coeffs.shape[2]).astype(jnp.float32), precision=HIGH)


def lower_level(transfer, coeffs):
    parents = coeffs.shape[0]
    basis_size = transfer.shape[1]
    result = jnp.einsum("cirk,ckf->cirf", transfer.reshape(parents, 8, basis_size, basis_size).astype(jnp.float32), coeffs.astype(jnp.float32), precision=HIGH)
    return result.reshape(parents * 8, basis_size, coeffs.shape[2])


def reference(src_leaf, adj_leaf, up_leaf, up_mid, couple_leaf, couple_mid, couple_top, send_slots, leaf_list, mid_list, top_list):
    both_leaf = jnp.concatenate([src_leaf, adj_leaf], axis=2)
    both_mid = lift_level(up_leaf, both_leaf).astype(jnp.bfloat16)
    both_top = lift_level(up_mid, both_mid).astype(jnp.bfloat16)
    mid_src = both_mid[:, :, :NF]
    mid_adj = both_mid[:, :, NF:]
    top_src = both_top[:, :, :NF]
    top_adj = both_top[:, :, NF:]
    src_pool = jnp.concatenate([src_leaf.reshape(PEERS, LEAF_DEV, R, NF), mid_src.reshape(PEERS, MID_DEV, R, NF)], axis=1)

    def device_step(adj_total, device_index):
        def coupled(slots, blocks, adj_own, adj_total):
            owner_dev = slots // CAP
            slot_pos = slots % CAP
            pool_index = send_slots[owner_dev, device_index, slot_pos]
            partners = src_pool[owner_dev, pool_index].astype(jnp.float32)
            near = jnp.einsum("ikrs,iksf->irf", blocks, partners, precision=HIGH)
            contrib = jnp.einsum("ikrs,irf->iksf", blocks, adj_own, precision=HIGH)
            dest = (owner_dev * POOL + pool_index).reshape(-1)
            adj_total = adj_total.at[dest].add(contrib.reshape(-1, R * NA))
            return near, adj_total

        leaf_slots = lax.dynamic_slice_in_dim(leaf_list, device_index * LEAF_DEV, LEAF_DEV, 0)
        mid_slots = lax.dynamic_slice_in_dim(mid_list, device_index * MID_DEV, MID_DEV, 0)
        leaf_blocks = lax.dynamic_slice_in_dim(couple_leaf, device_index * LEAF_DEV, LEAF_DEV, 0).astype(jnp.float32)
        mid_blocks = lax.dynamic_slice_in_dim(couple_mid, device_index * MID_DEV, MID_DEV, 0).astype(jnp.float32)
        leaf_own = lax.dynamic_slice_in_dim(adj_leaf, device_index * LEAF_DEV, LEAF_DEV, 0).astype(jnp.float32)
        mid_own = lax.dynamic_slice_in_dim(mid_adj, device_index * MID_DEV, MID_DEV, 0).astype(jnp.float32)
        leaf_near, adj_total = coupled(leaf_slots, leaf_blocks, leaf_own, adj_total)
        mid_near, adj_total = coupled(mid_slots, mid_blocks, mid_own, adj_total)
        return adj_total, (leaf_near, mid_near)

    start_total = jnp.zeros((PEERS * POOL, R * NA), jnp.float32)
    adj_total, near_parts = lax.scan(device_step, start_total, jnp.arange(PEERS, dtype=jnp.int32))
    leaf_near = near_parts[0].reshape(NC3, R, NF)
    mid_near = near_parts[1].reshape(NC2, R, NF)
    adj_pool = adj_total.reshape(PEERS, POOL, R, NA)
    leaf_far = adj_pool[:, :LEAF_DEV].reshape(NC3, R, NA)
    mid_far = adj_pool[:, LEAF_DEV:].reshape(NC2, R, NA)

    top_blocks = couple_top.astype(jnp.float32)
    top_near = jnp.einsum("ikrs,iksf->irf", top_blocks, top_src[top_list].astype(jnp.float32), precision=HIGH)
    top_contrib = jnp.einsum("ikrs,irf->iksf", top_blocks, top_adj.astype(jnp.float32), precision=HIGH)
    top_far = jnp.zeros((NC1, R * NA), jnp.float32).at[top_list.reshape(-1)].add(top_contrib.reshape(-1, R * NA)).reshape(NC1, R, NA)
    top_local = jnp.concatenate([top_near, top_far], axis=2).astype(jnp.bfloat16)
    mid_local = (jnp.concatenate([mid_near, mid_far], axis=2) + lower_level(up_mid, top_local)).astype(jnp.bfloat16)
    leaf_total = jnp.concatenate([leaf_near, leaf_far], axis=2) + lower_level(up_leaf, mid_local)
    return leaf_total[:, :, :NF].astype(jnp.bfloat16), leaf_total[:, :, NF:].astype(jnp.bfloat16)
```

```python
import functools

import jax
import jax.numpy as jnp
from jax import lax
from jax.experimental import pallas as pl
from jax.experimental.pallas import tpu as pltpu
from jax.sharding import PartitionSpec as P

BF16 = jnp.bfloat16
F32 = jnp.float32


def mul(x, y):
    return lax.dot_general(x, y, (((1,), (0,)), ((), ())), preferred_element_type=F32)


def mul_t(x, y):
    return lax.dot_general(x, y, (((1,), (1,)), ((), ())), preferred_element_type=F32)


def side(*blocks):
    return jnp.concatenate(blocks, axis=1)


def fold(x):
    half = x.shape[0] // 2
    return side(x[:half], x[half:])


def unfold(x):
    half = x.shape[1] // 2
    return jnp.concatenate([x[:, :half], x[:, half:]], axis=0)


def lift(rows, up, c):
    size, rank = up.shape[1:]
    return mul(side(*[rows[8 * c + i] for i in range(8)]), up[8 * c : 8 * c + 8].reshape(8 * size, rank))


def turn(up, c, eye):
    rank, size = up.shape[1:]
    return mul_t(eye, up[8 * c : 8 * c + 8].reshape(8 * rank, size)).astype(BF16)


def lower(local, down):
    rank = down.shape[0]
    below = mul(local, down)
    return [below[:, i * rank : (i + 1) * rank] for i in range(8)]


def lift_kernel(
    slots_in, src_in, up_leaf_in, up_mid_in, out, slots, src, up_leaf, up_mid, message, mid_src, tile, sems
):
    leaves, nf, rank = src.shape
    mids = up_mid.shape[0]
    parts = 4
    part = out.shape[0] // parts
    fetch_src = pltpu.make_async_copy(src_in, src, sems.at[0])
    fetch_leaf = pltpu.make_async_copy(up_leaf_in, up_leaf, sems.at[1])
    fetch_mid = pltpu.make_async_copy(up_mid_in, up_mid, sems.at[2])
    fetch_slots = pltpu.make_async_copy(slots_in, slots, sems.at[7])
    fetch_slots.start()
    fetch_src.start()
    fetch_leaf.start()
    fetch_mid.start()

    def pack_leaf(p, carry):
        message[p, :nf] = side(src[slots[0, 0, p]], src[slots[1, 0, p]])
        return carry

    fetch_slots.wait()
    fetch_src.wait()
    lax.fori_loop(0, out.shape[0], pack_leaf, 0, unroll=16)
    fetch_leaf.wait()
    for c in range(mids):
        mid_src[c] = lift(src, up_leaf, c).astype(BF16)
    fetch_mid.wait()
    top_src = lift(mid_src, up_mid, 0).astype(BF16)
    for core in range(2):
        top_half = fold(top_src[core * nf // 2 : (core + 1) * nf // 2])
        for c in range(mids):
            tile[core, c] = jnp.concatenate([fold(mid_src[c]), top_half], axis=0)

    sends = []
    for n in range(parts):
        for core in range(2):

            def pack_rest(i, carry):
                p = n * part + core * (part // 2) + i
                message[p, nf:] = tile[core, slots[2, 0, p] - leaves]
                return carry

            lax.fori_loop(0, part // 2, pack_rest, 0, unroll=16)
        place = pl.ds(n * part, part)
        sends.append(pltpu.make_async_copy(message.at[place], out.at[place], sems.at[3 + n]))
        sends[n].start()
    wait_all(sends)


def top_kernel(top_list, adj, up_leaf, up_mid, couple_top, outgoing, mid_adj, own, other, total):
    nf, rank = adj.shape[1:]
    half = nf // 2
    total[...] = jnp.zeros(total.shape, F32)
    for c in range(mid_adj.shape[0]):
        mid_adj[c] = lift(adj, up_leaf, c).astype(BF16)
    top_adj = lift(mid_adj, up_mid, 0).astype(BF16)
    for k in range(0, couple_top.shape[1], 4):
        terms = mul(top_adj, side(*[couple_top[0, k + j] for j in range(4)]))
        for j in range(4):
            term = terms[:, j * rank : (j + 1) * rank]
            e = top_list[0, k + j]
            sums = [total[core, e] + fold(term[core * half : (core + 1) * half]) for core in range(2)]
            for core in range(2):
                total[core, e] = sums[core]
    core = lax.axis_index("grp") % 2
    own[...] = total[core]
    other[...] = total[1 - core].astype(BF16)


def start_all(copies):
    for copy in copies:
        copy.start()


def wait_all(copies):
    for copy in copies:
        copy.wait()


def adjoint_kernel(
    leaf_list_in,
    mid_list_in,
    adj_in,
    mid_adj_in,
    couple_leaf_in,
    couple_mid_in,
    out,
    leaf_pairs_out,
    mid_pairs_out,
    leaf_list,
    mid_list,
    adj,
    mid_adj,
    couple_leaf,
    couple_mid,
    leaf_pairs,
    mid_pairs,
    message,
    even,
    odd,
    sems,
    leaf_sems,
    pair_sems,
    out_sems,
):
    width, rank = couple_leaf.shape[1:3]
    nf = adj.shape[1]
    half = nf // 2
    steps = leaf_sems.shape[0]
    chunk = adj.shape[0] // steps
    is_low = lax.broadcasted_iota(jnp.int32, (half, 2 * rank), 1) < rank

    def leaves(step):
        return pl.ds(pl.multiple_of(step * chunk, chunk), chunk)

    def fetch(step):
        return pltpu.make_async_copy(
            couple_leaf_in.at[leaves(step)], couple_leaf.at[leaves(step)], leaf_sems.at[step]
        )

    def keep_pairs(step):
        return pltpu.make_async_copy(
            leaf_pairs.at[leaves(step)], leaf_pairs_out.at[leaves(step)], pair_sems.at[step]
        )

    fetches = [
        pltpu.make_async_copy(leaf_list_in, leaf_list, sems.at[0]),
        pltpu.make_async_copy(mid_list_in, mid_list, sems.at[1]),
        pltpu.make_async_copy(adj_in, adj, sems.at[2]),
        pltpu.make_async_copy(mid_adj_in, mid_adj, sems.at[3]),
    ]
    fetch_mid = pltpu.make_async_copy(couple_mid_in, couple_mid, sems.at[4])
    keep_mid = pltpu.make_async_copy(mid_pairs, mid_pairs_out, sems.at[5])
    start_all(fetches)
    for step in range(steps):
        fetch(step).start()
    fetch_mid.start()

    def clear(e, carry):
        even[e] = jnp.zeros((half, 2 * rank), F32)
        odd[e] = jnp.zeros((half, 2 * rank), F32)
        return carry

    lax.fori_loop(0, even.shape[0], clear, 0, unroll=8)
    wait_all(fetches)

    def scatter(row, blocks, slot, keep):
        for k in range(0, width, 4):
            pairs = [side(blocks(k), blocks(k + 1)), side(blocks(k + 2), blocks(k + 3))]
            terms = mul(row, side(*pairs))
            for j in range(2):
                keep(k // 2 + j, pairs[j])
                pair = terms[:, 2 * j * rank : 2 * (j + 1) * rank]
                crossed = pltpu.roll(pair[half:], rank, 1)
                e, o = slot(k + 2 * j), slot(k + 2 * j + 1)
                even_sum = even[e] + jnp.where(is_low, pair[:half], crossed)
                odd_sum = odd[o] + jnp.where(is_low, crossed, pair[:half])
                even[e] = even_sum
                odd[o] = odd_sum

    def leaf_step(step, carry):
        fetch(step).wait()
        for a in range(chunk):
            g = step * chunk + a

            def keep(k, pair):
                leaf_pairs[g, k] = pair

            scatter(adj[g], lambda k: couple_leaf[g, k], lambda k: leaf_list[k, g], keep)
        keep_pairs(step).start()
        return carry

    lax.fori_loop(0, steps, leaf_step, 0)
    fetch_mid.wait()
    for c in range(mid_adj.shape[0]):

        def keep(k, pair):
            mid_pairs[c, k] = pair

        scatter(mid_adj[c], lambda k: couple_mid[c, k], lambda k: mid_list[c, k], keep)
    keep_mid.start()

    def pack(p, carry):
        for s in range(3):
            e = 3 * p + s
            message[p, s * half : (s + 1) * half] = (even[e] + pltpu.roll(odd[e], rank, 1)).astype(BF16)
        return carry

    parts = out_sems.shape[0]
    part = out.shape[0] // parts
    sends = []
    for n in range(parts):
        lax.fori_loop(n * part, (n + 1) * part, pack, 0, unroll=8)
        place = pl.ds(n * part, part)
        sends.append(pltpu.make_async_copy(message.at[place], out.at[place], out_sems.at[n]))
        sends[n].start()
    for step in range(steps):
        keep_pairs(step).wait()
    keep_mid.wait()
    wait_all(sends)


def gather(pairs, partner):
    near = 0
    for k in range(0, 16, 4):
        near += mul_t(side(*[partner(k + j) for j in range(4)]), side(pairs(k // 2), pairs(k // 2 + 1)))
    return near


def forward_kernel(
    leaf_list_in,
    mid_list_in,
    arrived_in,
    leaf_pairs_in,
    mid_pairs_in,
    leaf_near_out,
    mid_near_out,
    leaf_list,
    mid_list,
    arrived,
    leaf_pairs,
    mid_pairs,
    leaf_near,
    mid_near,
    coeff,
    sems,
    arrived_sems,
    leaf_sems,
    near_sems,
):
    leaves, nf, rank = leaf_near.shape
    steps = leaf_sems.shape[0]
    chunk = leaves // steps
    parts = arrived_sems.shape[0]
    part = arrived.shape[0] // parts

    def place(step):
        return pl.ds(pl.multiple_of(step * chunk, chunk), chunk)

    def fetch(step):
        return pltpu.make_async_copy(leaf_pairs_in.at[place(step)], leaf_pairs.at[place(step)], leaf_sems.at[step])

    def keep(step):
        return pltpu.make_async_copy(leaf_near.at[place(step)], leaf_near_out.at[place(step)], near_sems.at[step])

    lists = [
        pltpu.make_async_copy(leaf_list_in, leaf_list, sems.at[0]),
        pltpu.make_async_copy(mid_list_in, mid_list, sems.at[1]),
    ]
    messages = []
    for n in range(parts):
        rows_n = pl.ds(n * part, part)
        messages.append(pltpu.make_async_copy(arrived_in.at[rows_n], arrived.at[rows_n], arrived_sems.at[n]))
    fetch_mid = pltpu.make_async_copy(mid_pairs_in, mid_pairs, sems.at[2])
    keep_mid = pltpu.make_async_copy(mid_near, mid_near_out, sems.at[3])
    start_all(messages)
    start_all(lists)
    for step in range(steps):
        fetch(step).start()
    fetch_mid.start()

    def unpack(p, carry):
        pair = arrived[p, :nf]
        coeff[3 * p] = pair[:, :rank]
        coeff[3 * p + 1] = pair[:, rank:]
        coeff[3 * p + 2] = unfold(arrived[p, nf : nf + nf // 2])
        return carry

    for n in range(parts):
        messages[n].wait()
        lax.fori_loop(n * part, (n + 1) * part, unpack, 0, unroll=8)
    wait_all(lists)

    def leaf_step(step, carry):
        fetch(step).wait()
        for a in range(chunk):
            g = step * chunk + a
            leaf_near[g] = gather(lambda k: leaf_pairs[g, k], lambda k: coeff[leaf_list[k, g]])
        keep(step).start()
        return carry

    lax.fori_loop(0, steps, leaf_step, 0)
    fetch_mid.wait()
    for c in range(mid_near.shape[0]):
        mid_near[c] = gather(lambda k: mid_pairs[c, k], lambda k: coeff[mid_list[c, k]])
    keep_mid.start()
    for step in range(steps):
        keep(step).wait()
    keep_mid.wait()


def finish_kernel(
    top_list, own_half, other_half, leaf_near, mid_near, up_leaf, up_mid, couple_top, forward, down_leaf, down_mid
):
    nf, rank = forward.shape[1:]
    shape = (rank, rank)
    eye = (lax.broadcasted_iota(jnp.int32, shape, 0) == lax.broadcasted_iota(jnp.int32, shape, 1)).astype(BF16)

    def partner(k):
        j = top_list[0, k]
        return jnp.concatenate([unfold(own_half[j]), unfold(other_half[j])], axis=0)

    near = gather(lambda k: side(couple_top[0, 2 * k], couple_top[0, 2 * k + 1]), partner)
    swapped = jnp.concatenate([near[nf // 2 :], near[: nf // 2]], axis=0)
    core = lax.axis_index("grp") % 2
    down_mid[...] = turn(up_mid, 0, eye)
    below_top = lower(jnp.where(core == 0, near, swapped).astype(BF16), down_mid[...])
    for c in range(mid_near.shape[0]):
        down = turn(up_leaf, c, eye)
        down_leaf[c] = down
        below = lower((mid_near[c] + below_top[c]).astype(BF16), down)
        for i in range(8):
            forward[8 * c + i] = (leaf_near[8 * c + i] + below[i]).astype(BF16)


def lower_kernel(
    slots_in,
    returned_in,
    down_leaf_in,
    down_mid_in,
    out,
    slots,
    returned,
    down_leaf,
    down_mid,
    adjoint,
    even,
    odd,
    even_mid,
    odd_mid,
    sems,
):
    leaves, nf, rank = adjoint.shape
    mids = down_leaf.shape[0]
    part = returned.shape[0] // 4
    fetches = []
    for n in range(4):
        place = pl.ds(n * part, part)
        fetches.append(pltpu.make_async_copy(returned_in.at[place], returned.at[place], sems.at[n]))
    fetch_leaf = pltpu.make_async_copy(down_leaf_in, down_leaf, sems.at[4])
    fetch_mid = pltpu.make_async_copy(down_mid_in, down_mid, sems.at[5])
    fetch_slots = pltpu.make_async_copy(slots_in, slots, sems.at[14])
    fetch_slots.start()
    start_all(fetches)
    fetch_mid.start()
    fetch_leaf.start()
    for far in (even, odd, even_mid, odd_mid):
        far[...] = jnp.zeros(far.shape, F32)
    half = nf // 2

    def collect(first, i, top):
        sums = []
        for p, far, far_mid in ((first + 2 * i, even, even_mid), (first + 2 * i + 1, odd, odd_mid)):
            for s, held in ((0, far), (1, far), (2, far_mid)):
                u = slots[s, 0, p] - (leaves if s == 2 else 0)
                sums.append((held, u, held[u] + returned[p, s * half : (s + 1) * half].astype(F32)))
            top += returned[p, 3 * half :].astype(F32)
        for held, u, value in sums:
            held[u] = value
        return top

    fetch_slots.wait()
    tops = [jnp.zeros((half // 2, 2 * rank), F32)] * 2
    for n in range(4):
        fetches[n].wait()
        for core in range(2):
            first = n * part + core * (part // 2)
            tops[core] = lax.fori_loop(0, part // 4, functools.partial(collect, first), tops[core], unroll=True)
    fars = [unfold(even_mid[c] + odd_mid[c]) for c in range(mids)]
    top_far = jnp.concatenate([unfold(tops[0]), unfold(tops[1])], axis=0)
    fetch_mid.wait()
    below_top = lower(top_far.astype(BF16), down_mid[...])
    fetch_leaf.wait()
    sends = []
    for c in range(mids):
        below = lower((fars[c] + below_top[c]).astype(BF16), down_leaf[c])
        for i in range(8):
            a = c * 8 + i
            adjoint[a] = (unfold(even[a] + odd[a]) + below[i]).astype(BF16)
        place = pl.ds(8 * c, 8)
        sends.append(pltpu.make_async_copy(adjoint.at[place], out.at[place], sems.at[6 + c]))
        sends[c].start()
    wait_all(sends)


SMEM = pl.BlockSpec(memory_space=pltpu.SMEM)
VMEM = pl.BlockSpec(memory_space=pltpu.VMEM)
HBM = pl.BlockSpec(memory_space=pl.ANY)


def exchange(x):
    return lax.all_to_all(x, ("grp", "dev"), split_axis=0, concat_axis=0, tiled=True)


def swap(x):
    return lax.ppermute(x, "grp", [(g, g ^ 1) for g in range(lax.axis_size("grp"))])


def on_device(
    src_leaf,
    adj_leaf,
    up_leaf,
    up_mid,
    couple_leaf,
    couple_mid,
    couple_top,
    send_slots,
    leaf_list,
    mid_list,
    top_list,
):
    leaves, rank, nf = src_leaf.shape
    mids = up_mid.shape[0]
    peers = send_slots.shape[1]
    width = couple_leaf.shape[1]
    steps = mids
    src = jnp.swapaxes(src_leaf, 1, 2)
    adj = jnp.swapaxes(adj_leaf, 1, 2)
    slots = jnp.transpose(send_slots, (2, 0, 1))
    leaf_slots = leaf_list.T
    message = (peers, 7 * nf // 4, 2 * rank)
    half_top = (peers, nf // 4, 2 * rank)
    shape = jax.ShapeDtypeStruct
    params = pltpu.CompilerParams(vmem_limit_bytes=66000000)
    small = pl.CostEstimate(flops=10**6, bytes_accessed=10**5, transcendentals=0)

    outgoing = pl.pallas_call(
        lift_kernel,
        out_shape=shape(message, BF16),
        in_specs=[HBM] * 4,
        out_specs=HBM,
        scratch_shapes=[
            pltpu.SMEM(slots.shape, jnp.int32),
            pltpu.VMEM((leaves, nf, rank), BF16),
            pltpu.VMEM((leaves, rank, rank), BF16),
            pltpu.VMEM((mids, rank, rank), BF16),
            pltpu.VMEM(message, BF16),
            pltpu.VMEM((mids, nf, rank), BF16),
            pltpu.VMEM((2, mids, 3 * nf // 4, 2 * rank), BF16),
            pltpu.SemaphoreType.DMA((8,)),
        ],
        compiler_params=params,
        name="lift",
    )(slots, src, up_leaf, up_mid)
    arrived = exchange(outgoing)

    leaf_pairs_shape = (leaves, width // 2, rank, 2 * rank)
    mid_pairs_shape = (mids, width // 2, rank, 2 * rank)
    mid_adj, own_terms, other_terms = pl.pallas_call(
        top_kernel,
        out_shape=(shape((mids, nf, rank), BF16), shape(half_top, F32), shape(half_top, BF16)),
        in_specs=[SMEM] + [VMEM] * 4 + [HBM],
        out_specs=(VMEM, VMEM, VMEM),
        scratch_shapes=[pltpu.VMEM((2,) + half_top, F32)],
        compiler_params=params,
        cost_estimate=small,
        name="top",
    )(top_list, adj, up_leaf, up_mid, couple_top, outgoing)
    swapped_terms = swap(other_terms)
    per_slot, leaf_pairs, mid_pairs = pl.pallas_call(
        adjoint_kernel,
        out_shape=(shape(message, BF16), shape(leaf_pairs_shape, BF16), shape(mid_pairs_shape, BF16)),
        in_specs=[HBM] * 6,
        out_specs=(HBM, HBM, HBM),
        scratch_shapes=[
            pltpu.SMEM(leaf_slots.shape, jnp.int32),
            pltpu.SMEM(mid_list.shape, jnp.int32),
            pltpu.VMEM(adj.shape, BF16),
            pltpu.VMEM(mid_adj.shape, BF16),
            pltpu.VMEM(couple_leaf.shape, BF16),
            pltpu.VMEM(couple_mid.shape, BF16),
            pltpu.VMEM(leaf_pairs_shape, BF16),
            pltpu.VMEM(mid_pairs_shape, BF16),
            pltpu.VMEM(message, BF16),
            pltpu.VMEM((3 * peers, nf // 2, 2 * rank), F32),
            pltpu.VMEM((3 * peers, nf // 2, 2 * rank), F32),
            pltpu.SemaphoreType.DMA((6,)),
            pltpu.SemaphoreType.DMA((steps,)),
            pltpu.SemaphoreType.DMA((steps,)),
            pltpu.SemaphoreType.DMA((4,)),
        ],
        compiler_params=params,
        cost_estimate=small,
        name="adjoint",
    )(leaf_slots, mid_list, adj, mid_adj, couple_leaf, couple_mid)
    top_terms = (own_terms + swapped_terms.astype(F32)).astype(BF16)
    returned = exchange(lax.dynamic_update_slice(per_slot, top_terms, (0, 3 * nf // 2, 0)))

    own_half = arrived[:, 3 * nf // 2 :]
    other_half = swap(own_half)
    leaf_near, mid_near = pl.pallas_call(
        forward_kernel,
        out_shape=(shape((leaves, nf, rank), F32), shape((mids, nf, rank), F32)),
        in_specs=[HBM] * 5,
        out_specs=(HBM, HBM),
        scratch_shapes=[
            pltpu.SMEM(leaf_slots.shape, jnp.int32),
            pltpu.SMEM(mid_list.shape, jnp.int32),
            pltpu.VMEM(message, BF16),
            pltpu.VMEM(leaf_pairs_shape, BF16),
            pltpu.VMEM(mid_pairs_shape, BF16),
            pltpu.VMEM((leaves, nf, rank), F32),
            pltpu.VMEM((mids, nf, rank), F32),
            pltpu.VMEM((3 * peers, nf, rank), BF16),
            pltpu.SemaphoreType.DMA((4,)),
            pltpu.SemaphoreType.DMA((4,)),
            pltpu.SemaphoreType.DMA((steps,)),
            pltpu.SemaphoreType.DMA((steps,)),
        ],
        compiler_params=params,
        cost_estimate=small,
        name="forward",
    )(leaf_slots, mid_list, arrived, leaf_pairs, mid_pairs)
    forward, down_leaf, down_mid = pl.pallas_call(
        finish_kernel,
        out_shape=(
            shape((leaves, nf, rank), BF16),
            shape((mids, rank, 8 * rank), BF16),
            shape((rank, 8 * rank), BF16),
        ),
        in_specs=[SMEM] + [VMEM] * 7,
        out_specs=(VMEM, VMEM, VMEM),
        compiler_params=params,
        cost_estimate=small,
        name="finish",
    )(top_list, own_half, other_half, leaf_near, mid_near, up_leaf, up_mid, couple_top)

    adjoint = pl.pallas_call(
        lower_kernel,
        out_shape=shape((leaves, nf, rank), BF16),
        in_specs=[HBM] * 4,
        out_specs=HBM,
        scratch_shapes=[
            pltpu.SMEM(slots.shape, jnp.int32),
            pltpu.VMEM(message, BF16),
            pltpu.VMEM((mids, rank, 8 * rank), BF16),
            pltpu.VMEM((rank, 8 * rank), BF16),
            pltpu.VMEM((leaves, nf, rank), BF16),
            pltpu.VMEM((leaves, nf // 2, 2 * rank), F32),
            pltpu.VMEM((leaves, nf // 2, 2 * rank), F32),
            pltpu.VMEM((mids, nf // 2, 2 * rank), F32),
            pltpu.VMEM((mids, nf // 2, 2 * rank), F32),
            pltpu.SemaphoreType.DMA((15,)),
        ],
        compiler_params=params,
        name="lower",
    )(slots, returned, down_leaf, down_mid)
    return jnp.swapaxes(forward, 1, 2), jnp.swapaxes(adjoint, 1, 2)


def solution(mesh):
    placed = (
        P(("grp", "dev"), None, None),
        P(("grp", "dev"), None, None),
        P(("grp", "dev"), None, None),
        P(("grp", "dev"), None, None),
        P(("grp", "dev"), None, None, None),
        P(("grp", "dev"), None, None, None),
        P(("grp", "dev"), None, None, None),
        P(("grp", "dev"), None, None),
        P(("grp", "dev"), None),
        P(("grp", "dev"), None),
        P(("grp", "dev"), None),
    )
    return jax.shard_map(
        on_device,
        mesh=mesh,
        in_specs=placed,
        out_specs=(P(("grp", "dev"), None, None), P(("grp", "dev"), None, None)),
        check_vma=False,
    )
```

```python
import jax
import jax.numpy as jnp
from jax import lax
from jax.experimental import pallas as pl
from jax.experimental.pallas import tpu as pltpu
from jax.sharding import PartitionSpec as P

BF16 = jnp.bfloat16
F32 = jnp.float32


def mul(x, y):
    return lax.dot_general(x, y, (((1,), (0,)), ((), ())), preferred_element_type=F32)


def mul_t(x, y):
    return lax.dot_general(x, y, (((1,), (1,)), ((), ())), preferred_element_type=F32)


def side(*blocks):
    return jnp.concatenate(blocks, axis=1)


def fold(x):
    half = x.shape[0] // 2
    return side(x[:half], x[half:])


def unfold(x):
    half = x.shape[1] // 2
    return jnp.concatenate([x[:, :half], x[:, half:]], axis=0)


def lift(rows, up, c):
    size, rank = up.shape[1:]
    return mul(side(*[rows[8 * c + i] for i in range(8)]), up[8 * c : 8 * c + 8].reshape(8 * size, rank))


def turn(up, c, eye):
    rank, size = up.shape[1:]
    return mul_t(eye, up[8 * c : 8 * c + 8].reshape(8 * rank, size)).astype(BF16)


def lower(local, down):
    rank = down.shape[0]
    below = mul(local, down)
    return [below[:, i * rank : (i + 1) * rank] for i in range(8)]


def lift_kernel(
    slots_in, src_in, up_leaf_in, up_mid_in, out, slots, src, up_leaf, up_mid, message, mid_src, tile, sems
):
    leaves, nf, rank = src.shape
    mids = up_mid.shape[0]
    parts = 4
    part = out.shape[0] // parts
    fetch_src = pltpu.make_async_copy(src_in, src, sems.at[0])
    fetch_leaf = pltpu.make_async_copy(up_leaf_in, up_leaf, sems.at[1])
    fetch_mid = pltpu.make_async_copy(up_mid_in, up_mid, sems.at[2])
    fetch_slots = pltpu.make_async_copy(slots_in, slots, sems.at[7])
    fetch_slots.start()
    fetch_src.start()
    fetch_leaf.start()
    fetch_mid.start()

    def pack_leaf(p, carry):
        message[p, :nf] = side(src[slots[0, 0, p]], src[slots[1, 0, p]])
        return carry

    fetch_slots.wait()
    fetch_src.wait()
    lax.fori_loop(0, out.shape[0], pack_leaf, 0, unroll=16)
    fetch_leaf.wait()
    for c in range(mids):
        mid_src[c] = lift(src, up_leaf, c).astype(BF16)
    fetch_mid.wait()
    top_src = lift(mid_src, up_mid, 0).astype(BF16)
    for core in range(2):
        top_half = fold(top_src[core * nf // 2 : (core + 1) * nf // 2])
        for c in range(mids):
            tile[core, c] = jnp.concatenate([fold(mid_src[c]), top_half], axis=0)

    sends = []
    for n in range(parts):
        for core in range(2):

            def pack_rest(i, carry):
                p = n * part + core * (part // 2) + i
                message[p, nf:] = tile[core, slots[2, 0, p] - leaves]
                return carry

            lax.fori_loop(0, part // 2, pack_rest, 0, unroll=16)
        place = pl.ds(n * part, part)
        sends.append(pltpu.make_async_copy(message.at[place], out.at[place], sems.at[3 + n]))
        sends[n].start()
    wait_all(sends)


def device_of(i, core):
    return (i >> 4) * 32 + core * 16 + (i & 15)


def top_kernel(top_list, adj, up_leaf, up_mid, couple_top, outgoing, mid_adj, own, other, total):
    rank = adj.shape[2]
    total[...] = jnp.zeros(total.shape, F32)
    for c in range(mid_adj.shape[0]):
        mid_adj[c] = lift(adj, up_leaf, c).astype(BF16)
    top_adj = lift(mid_adj, up_mid, 0).astype(BF16)
    core = lax.axis_index("grp") & 1
    for k in range(0, couple_top.shape[1], 4):
        terms = mul(top_adj, side(*[couple_top[0, k + j] for j in range(4)]))
        for j in range(4):
            p = top_list[0, k + j]
            place = ((p >> 4) & 1) ^ core
            total[place, (p >> 5) * 16 + (p & 15)] += fold(terms[:, j * rank : (j + 1) * rank])
    own[...] = total[0]
    other[...] = total[1].astype(BF16)


def start_all(copies):
    for copy in copies:
        copy.start()


def wait_all(copies):
    for copy in copies:
        copy.wait()


def adjoint_kernel(
    leaf_list_in,
    mid_list_in,
    adj_in,
    mid_adj_in,
    couple_leaf_in,
    couple_mid_in,
    out,
    other,
    leaf_list,
    mid_list,
    adj,
    mid_adj,
    couple_leaf,
    couple_mid,
    message,
    even,
    odd,
    sems,
    leaf_sems,
    out_sems,
):
    width, rank = couple_leaf.shape[1:3]
    nf = adj.shape[1]
    half = nf // 2
    steps = leaf_sems.shape[0]
    chunk = adj.shape[0] // steps
    is_low = lax.broadcasted_iota(jnp.int32, (half, 2 * rank), 1) < rank

    def fetch(step):
        place = pl.ds(pl.multiple_of(step * chunk, chunk), chunk)
        return pltpu.make_async_copy(couple_leaf_in.at[place], couple_leaf.at[place], leaf_sems.at[step])

    fetches = [
        pltpu.make_async_copy(leaf_list_in, leaf_list, sems.at[0]),
        pltpu.make_async_copy(mid_list_in, mid_list, sems.at[1]),
        pltpu.make_async_copy(adj_in, adj, sems.at[2]),
        pltpu.make_async_copy(mid_adj_in, mid_adj, sems.at[3]),
    ]
    fetch_mid = pltpu.make_async_copy(couple_mid_in, couple_mid, sems.at[4])
    start_all(fetches)
    for step in range(steps):
        fetch(step).start()
    fetch_mid.start()

    def clear(e, carry):
        even[e] = jnp.zeros((half, 2 * rank), F32)
        odd[e] = jnp.zeros((half, 2 * rank), F32)
        return carry

    lax.fori_loop(0, even.shape[0], clear, 0, unroll=8)
    wait_all(fetches)

    def scatter(row, blocks, slot):
        for k in range(0, width, 4):
            terms = mul(row, side(*[blocks(k + j) for j in range(4)]))
            for j in range(2):
                pair = terms[:, 2 * j * rank : 2 * (j + 1) * rank]
                crossed = pltpu.roll(pair[half:], rank, 1)
                e, o = slot(k + 2 * j), slot(k + 2 * j + 1)
                even_sum = even[e] + jnp.where(is_low, pair[:half], crossed)
                odd_sum = odd[o] + jnp.where(is_low, crossed, pair[:half])
                even[e] = even_sum
                odd[o] = odd_sum

    def leaf_step(step, carry):
        fetch(step).wait()
        for a in range(chunk):
            g = step * chunk + a
            scatter(adj[g], lambda k: couple_leaf[g, k], lambda k: leaf_list[k, g])
        return carry

    lax.fori_loop(0, steps, leaf_step, 0)
    fetch_mid.wait()
    for c in range(mid_adj.shape[0]):
        scatter(mid_adj[c], lambda k: couple_mid[c, k], lambda k: mid_list[c, k])

    core = lax.axis_index("grp") & 1
    sends = []
    for place, target in ((1, other), (0, out)):

        def pack(i, carry):
            p = device_of(i, core ^ place)
            for s in range(3):
                e = 3 * p + s
                block = even[e] + pltpu.roll(odd[e], rank, 1)
                message[place, i, s * half : (s + 1) * half] = block.astype(BF16)
            return carry

        part = other.shape[0] // 2
        for n in range(2):
            lax.fori_loop(n * part, (n + 1) * part, pack, 0, unroll=8)
            rows = pl.ds(n * part, part)
            copy = pltpu.make_async_copy(
                message.at[place, rows], target.at[rows, pl.ds(0, 3 * half)], out_sems.at[2 * place + n]
            )
            copy.start()
            sends.append(copy)
    wait_all(sends)


def gather(blocks, partner):
    near = 0
    for k in range(0, 16, 4):
        near += mul_t(side(*[partner(k + j) for j in range(4)]), side(*[blocks(k + j) for j in range(4)]))
    return near


def forward_kernel(
    leaf_list_in,
    mid_list_in,
    arrived_in,
    couple_leaf_in,
    couple_mid_in,
    leaf_near_out,
    mid_near_out,
    leaf_list,
    mid_list,
    arrived,
    couple_leaf,
    couple_mid,
    leaf_near,
    mid_near,
    coeff,
    sems,
    arrived_sems,
    leaf_sems,
    near_sems,
):
    leaves, nf, rank = leaf_near.shape
    steps = leaf_sems.shape[0]
    chunk = leaves // steps
    parts = arrived_sems.shape[0]
    part = arrived.shape[0] // parts

    def place(step):
        return pl.ds(pl.multiple_of(step * chunk, chunk), chunk)

    def fetch(step):
        return pltpu.make_async_copy(couple_leaf_in.at[place(step)], couple_leaf.at[place(step)], leaf_sems.at[step])

    def keep(step):
        return pltpu.make_async_copy(leaf_near.at[place(step)], leaf_near_out.at[place(step)], near_sems.at[step])

    lists = [
        pltpu.make_async_copy(leaf_list_in, leaf_list, sems.at[0]),
        pltpu.make_async_copy(mid_list_in, mid_list, sems.at[1]),
    ]
    messages = []
    for n in range(parts):
        rows_n = pl.ds(n * part, part)
        messages.append(pltpu.make_async_copy(arrived_in.at[rows_n], arrived.at[rows_n], arrived_sems.at[n]))
    fetch_mid = pltpu.make_async_copy(couple_mid_in, couple_mid, sems.at[2])
    keep_mid = pltpu.make_async_copy(mid_near, mid_near_out, sems.at[3])
    start_all(messages)
    start_all(lists)
    for step in range(steps):
        fetch(step).start()
    fetch_mid.start()

    def unpack(p, carry):
        pair = arrived[p, :nf]
        coeff[3 * p] = pair[:, :rank]
        coeff[3 * p + 1] = pair[:, rank:]
        coeff[3 * p + 2] = unfold(arrived[p, nf : nf + nf // 2])
        return carry

    for n in range(parts):
        messages[n].wait()
        lax.fori_loop(n * part, (n + 1) * part, unpack, 0, unroll=8)
    wait_all(lists)

    def leaf_step(step, carry):
        fetch(step).wait()
        for a in range(chunk):
            g = step * chunk + a
            leaf_near[g] = gather(lambda k: couple_leaf[g, k], lambda k: coeff[leaf_list[k, g]])
        keep(step).start()
        return carry

    lax.fori_loop(0, steps, leaf_step, 0)
    fetch_mid.wait()
    for c in range(mid_near.shape[0]):
        mid_near[c] = gather(lambda k: couple_mid[c, k], lambda k: coeff[mid_list[c, k]])
    keep_mid.start()
    for step in range(steps):
        keep(step).wait()
    keep_mid.wait()


def finish_kernel(
    top_list, own_half, other_half, leaf_near, mid_near, up_leaf, up_mid, couple_top, forward, down_leaf, down_mid
):
    nf, rank = forward.shape[1:]
    shape = (rank, rank)
    eye = (lax.broadcasted_iota(jnp.int32, shape, 0) == lax.broadcasted_iota(jnp.int32, shape, 1)).astype(BF16)

    def partner(k):
        j = top_list[0, k]
        return jnp.concatenate([unfold(own_half[j]), unfold(other_half[j])], axis=0)

    near = gather(lambda k: couple_top[0, k], partner)
    swapped = jnp.concatenate([near[nf // 2 :], near[: nf // 2]], axis=0)
    core = lax.axis_index("grp") % 2
    down_mid[...] = turn(up_mid, 0, eye)
    below_top = lower(jnp.where(core == 0, near, swapped).astype(BF16), down_mid[...])
    for c in range(mid_near.shape[0]):
        down = turn(up_leaf, c, eye)
        down_leaf[c] = down
        below = lower((mid_near[c] + below_top[c]).astype(BF16), down)
        for i in range(8):
            forward[8 * c + i] = (leaf_near[8 * c + i] + below[i]).astype(BF16)


def lower_kernel(
    slots_in,
    returned_in,
    down_leaf_in,
    down_mid_in,
    out,
    slots,
    returned,
    down_leaf,
    down_mid,
    adjoint,
    even,
    odd,
    even_mid,
    odd_mid,
    sems,
):
    leaves, nf, rank = adjoint.shape
    mids = down_leaf.shape[0]
    part = returned.shape[0] // 4
    fetches = []
    for n in range(4):
        place = pl.ds(n * part, part)
        fetches.append(pltpu.make_async_copy(returned_in.at[place], returned.at[place], sems.at[n]))
    fetch_leaf = pltpu.make_async_copy(down_leaf_in, down_leaf, sems.at[4])
    fetch_mid = pltpu.make_async_copy(down_mid_in, down_mid, sems.at[5])
    fetch_slots = pltpu.make_async_copy(slots_in, slots, sems.at[14])
    fetch_slots.start()
    start_all(fetches)
    fetch_mid.start()
    fetch_leaf.start()
    for far in (even, odd, even_mid, odd_mid):
        far[...] = jnp.zeros(far.shape, F32)
    half = nf // 2
    core = lax.axis_index("grp") & 1

    def collect(i, top):
        sums = []
        for place, far, far_mid in ((0, even, even_mid), (1, odd, odd_mid)):
            p = device_of(i, core ^ place)
            for s, held in ((0, far), (1, far), (2, far_mid)):
                u = slots[s, 0, p] - (leaves if s == 2 else 0)
                first = (3 * place + s) * half
                sums.append((held, u, held[u] + returned[i, first : first + half].astype(F32)))
        for held, u, value in sums:
            held[u] = value
        return top + returned[i, 6 * half :].astype(F32)

    fetch_slots.wait()
    top = jnp.zeros((half, 2 * rank), F32)
    for n in range(4):
        fetches[n].wait()
        top = lax.fori_loop(n * part, (n + 1) * part, collect, top, unroll=8)
    fars = [unfold(even_mid[c] + odd_mid[c]) for c in range(mids)]
    fetch_mid.wait()
    below_top = lower(unfold(top).astype(BF16), down_mid[...])
    fetch_leaf.wait()
    sends = []
    for c in range(mids):
        below = lower((fars[c] + below_top[c]).astype(BF16), down_leaf[c])
        for i in range(8):
            a = c * 8 + i
            adjoint[a] = (unfold(even[a] + odd[a]) + below[i]).astype(BF16)
        place = pl.ds(8 * c, 8)
        sends.append(pltpu.make_async_copy(adjoint.at[place], out.at[place], sems.at[6 + c]))
        sends[c].start()
    wait_all(sends)


SMEM = pl.BlockSpec(memory_space=pltpu.SMEM)
VMEM = pl.BlockSpec(memory_space=pltpu.VMEM)
HBM = pl.BlockSpec(memory_space=pl.ANY)


def exchange(x):
    return lax.all_to_all(x, ("grp", "dev"), split_axis=0, concat_axis=0, tiled=True)


def swap(x):
    return lax.ppermute(x, "grp", [(g, g ^ 1) for g in range(lax.axis_size("grp"))])


def on_device(
    src_leaf,
    adj_leaf,
    up_leaf,
    up_mid,
    couple_leaf,
    couple_mid,
    couple_top,
    send_slots,
    leaf_list,
    mid_list,
    top_list,
):
    leaves, rank, nf = src_leaf.shape
    mids = up_mid.shape[0]
    peers = send_slots.shape[1]
    width = couple_leaf.shape[1]
    steps = mids
    src = jnp.swapaxes(src_leaf, 1, 2)
    adj = jnp.swapaxes(adj_leaf, 1, 2)
    slots = jnp.transpose(send_slots, (2, 0, 1))
    leaf_slots = leaf_list.T
    message = (peers, 7 * nf // 4, 2 * rank)
    chips = peers // 2
    second_message = (chips, 7 * nf // 2, 2 * rank)
    swapped_message = (chips, 3 * nf // 2, 2 * rank)
    top_shape = (chips, nf // 2, 2 * rank)
    shape = jax.ShapeDtypeStruct
    params = pltpu.CompilerParams(vmem_limit_bytes=66000000)
    small = pl.CostEstimate(flops=10**6, bytes_accessed=10**5, transcendentals=0)

    outgoing = pl.pallas_call(
        lift_kernel,
        out_shape=shape(message, BF16),
        in_specs=[HBM] * 4,
        out_specs=HBM,
        scratch_shapes=[
            pltpu.SMEM(slots.shape, jnp.int32),
            pltpu.VMEM((leaves, nf, rank), BF16),
            pltpu.VMEM((leaves, rank, rank), BF16),
            pltpu.VMEM((mids, rank, rank), BF16),
            pltpu.VMEM(message, BF16),
            pltpu.VMEM((mids, nf, rank), BF16),
            pltpu.VMEM((2, mids, 3 * nf // 4, 2 * rank), BF16),
            pltpu.SemaphoreType.DMA((8,)),
        ],
        compiler_params=params,
        name="lift",
    )(slots, src, up_leaf, up_mid)
    arrived = exchange(outgoing)

    mid_adj, own_terms, other_terms = pl.pallas_call(
        top_kernel,
        out_shape=(shape((mids, nf, rank), BF16), shape(top_shape, F32), shape(top_shape, BF16)),
        in_specs=[SMEM] + [VMEM] * 4 + [HBM],
        out_specs=(VMEM, VMEM, VMEM),
        scratch_shapes=[pltpu.VMEM((2,) + top_shape, F32)],
        compiler_params=params,
        cost_estimate=small,
        name="top",
    )(top_list, adj, up_leaf, up_mid, couple_top, outgoing)
    swapped_terms = swap(other_terms)
    per_slot, for_other = pl.pallas_call(
        adjoint_kernel,
        out_shape=(shape(second_message, BF16), shape(swapped_message, BF16)),
        in_specs=[HBM] * 6,
        out_specs=(HBM, HBM),
        scratch_shapes=[
            pltpu.SMEM(leaf_slots.shape, jnp.int32),
            pltpu.SMEM(mid_list.shape, jnp.int32),
            pltpu.VMEM(adj.shape, BF16),
            pltpu.VMEM(mid_adj.shape, BF16),
            pltpu.VMEM(couple_leaf.shape, BF16),
            pltpu.VMEM(couple_mid.shape, BF16),
            pltpu.VMEM((2,) + swapped_message, BF16),
            pltpu.VMEM((3 * peers, nf // 2, 2 * rank), F32),
            pltpu.VMEM((3 * peers, nf // 2, 2 * rank), F32),
            pltpu.SemaphoreType.DMA((5,)),
            pltpu.SemaphoreType.DMA((steps,)),
            pltpu.SemaphoreType.DMA((4,)),
        ],
        compiler_params=params,
        cost_estimate=small,
        name="adjoint",
    )(leaf_slots, mid_list, adj, mid_adj, couple_leaf, couple_mid)
    top_terms = (own_terms + swapped_terms.astype(F32)).astype(BF16)
    per_slot = lax.dynamic_update_slice(per_slot, swap(for_other), (0, 3 * nf // 2, 0))
    per_slot = lax.dynamic_update_slice(per_slot, top_terms, (0, 3 * nf, 0))
    same_core = [[device_of(i, core) for i in range(chips)] for core in range(2)]
    returned = lax.all_to_all(
        per_slot, ("grp", "dev"), split_axis=0, concat_axis=0, axis_index_groups=same_core, tiled=True
    )

    own_half = arrived[:, 3 * nf // 2 :]
    other_half = swap(own_half)
    leaf_near, mid_near = pl.pallas_call(
        forward_kernel,
        out_shape=(shape((leaves, nf, rank), F32), shape((mids, nf, rank), F32)),
        in_specs=[HBM] * 5,
        out_specs=(HBM, HBM),
        scratch_shapes=[
            pltpu.SMEM(leaf_slots.shape, jnp.int32),
            pltpu.SMEM(mid_list.shape, jnp.int32),
            pltpu.VMEM(message, BF16),
            pltpu.VMEM(couple_leaf.shape, BF16),
            pltpu.VMEM(couple_mid.shape, BF16),
            pltpu.VMEM((leaves, nf, rank), F32),
            pltpu.VMEM((mids, nf, rank), F32),
            pltpu.VMEM((3 * peers, nf, rank), BF16),
            pltpu.SemaphoreType.DMA((4,)),
            pltpu.SemaphoreType.DMA((4,)),
            pltpu.SemaphoreType.DMA((steps,)),
            pltpu.SemaphoreType.DMA((steps,)),
        ],
        compiler_params=params,
        cost_estimate=small,
        name="forward",
    )(leaf_slots, mid_list, arrived, couple_leaf, couple_mid)
    forward, down_leaf, down_mid = pl.pallas_call(
        finish_kernel,
        out_shape=(
            shape((leaves, nf, rank), BF16),
            shape((mids, rank, 8 * rank), BF16),
            shape((rank, 8 * rank), BF16),
        ),
        in_specs=[SMEM] + [VMEM] * 7,
        out_specs=(VMEM, VMEM, VMEM),
        compiler_params=params,
        cost_estimate=small,
        name="finish",
    )(top_list, own_half, other_half, leaf_near, mid_near, up_leaf, up_mid, couple_top)

    adjoint = pl.pallas_call(
        lower_kernel,
        out_shape=shape((leaves, nf, rank), BF16),
        in_specs=[HBM] * 4,
        out_specs=HBM,
        scratch_shapes=[
            pltpu.SMEM(slots.shape, jnp.int32),
            pltpu.VMEM(second_message, BF16),
            pltpu.VMEM((mids, rank, 8 * rank), BF16),
            pltpu.VMEM((rank, 8 * rank), BF16),
            pltpu.VMEM((leaves, nf, rank), BF16),
            pltpu.VMEM((leaves, nf // 2, 2 * rank), F32),
            pltpu.VMEM((leaves, nf // 2, 2 * rank), F32),
            pltpu.VMEM((mids, nf // 2, 2 * rank), F32),
            pltpu.VMEM((mids, nf // 2, 2 * rank), F32),
            pltpu.SemaphoreType.DMA((15,)),
        ],
        compiler_params=params,
        name="lower",
    )(slots, returned, down_leaf, down_mid)
    return jnp.swapaxes(forward, 1, 2), jnp.swapaxes(adjoint, 1, 2)


def solution(mesh):
    placed = (
        P(("grp", "dev"), None, None),
        P(("grp", "dev"), None, None),
        P(("grp", "dev"), None, None),
        P(("grp", "dev"), None, None),
        P(("grp", "dev"), None, None, None),
        P(("grp", "dev"), None, None, None),
        P(("grp", "dev"), None, None, None),
        P(("grp", "dev"), None, None),
        P(("grp", "dev"), None),
        P(("grp", "dev"), None),
        P(("grp", "dev"), None),
    )
    return jax.shard_map(
        on_device,
        mesh=mesh,
        in_specs=placed,
        out_specs=(P(("grp", "dev"), None, None), P(("grp", "dev"), None, None)),
        check_vma=False,
    )
```

```python
import jax
import jax.numpy as jnp
from jax import lax
from jax.experimental import pallas as pl
from jax.experimental.pallas import tpu as pltpu
from jax.sharding import PartitionSpec as P

BF16 = jnp.bfloat16
F32 = jnp.float32


def mul(x, y):
    return lax.dot_general(x, y, (((1,), (0,)), ((), ())), preferred_element_type=F32)


def mul_t(x, y):
    return lax.dot_general(x, y, (((1,), (1,)), ((), ())), preferred_element_type=F32)


def side(*blocks):
    return jnp.concatenate(blocks, axis=1)


def fold(x):
    half = x.shape[0] // 2
    return side(x[:half], x[half:])


def unfold(x):
    half = x.shape[1] // 2
    return jnp.concatenate([x[:, :half], x[:, half:]], axis=0)


def lift(rows, up, c):
    size, rank = up.shape[1:]
    return mul(side(*[rows[8 * c + i] for i in range(8)]), up[8 * c : 8 * c + 8].reshape(8 * size, rank))


def turn(up, c, eye):
    rank, size = up.shape[1:]
    return mul_t(eye, up[8 * c : 8 * c + 8].reshape(8 * rank, size)).astype(BF16)


def lower(local, down):
    rank = down.shape[0]
    below = mul(local, down)
    return [below[:, i * rank : (i + 1) * rank] for i in range(8)]


def device_of(i, core):
    return (i >> 4) * 32 + core * 16 + (i & 15)


def place_of(p):
    return (p >> 5) * 16 + (p & 15)


def lift_kernel(
    slots_in, src_in, up_leaf_in, up_mid_in, out, slots, src, up_leaf, up_mid, message, mid_src, tile, sems
):
    leaves, nf, rank = src.shape
    mids = up_mid.shape[0]
    half = nf // 2
    core = lax.axis_index("grp") & 1
    parts = 4
    part = out.shape[0] // parts
    fetch_src = pltpu.make_async_copy(src_in, src, sems.at[4])
    fetch_leaf = pltpu.make_async_copy(up_leaf_in, up_leaf, sems.at[5])
    fetch_mid = pltpu.make_async_copy(up_mid_in, up_mid, sems.at[6])
    fetch_slots = pltpu.make_async_copy(slots_in, slots, sems.at[7])
    fetch_slots.start()
    fetch_src.start()
    fetch_leaf.start()
    fetch_mid.start()

    def pack_leaf(i, carry):
        for place in range(2):
            p = device_of(i, core ^ place)
            first = 3 * half * place
            message[i, first : first + nf] = side(src[slots[0, 0, p]], src[slots[1, 0, p]])
        return carry

    fetch_slots.wait()
    fetch_src.wait()
    lax.fori_loop(0, out.shape[0], pack_leaf, 0, unroll=8)
    fetch_leaf.wait()
    for c in range(mids):
        mid_src[c] = lift(src, up_leaf, c).astype(BF16)
    fetch_mid.wait()
    top_src = fold(lift(mid_src, up_mid, 0).astype(BF16))
    for c in range(mids):
        tile[c] = jnp.concatenate([fold(mid_src[c]), top_src], axis=0)

    def pack_rest(i, carry):
        message[i, nf : 3 * half] = tile[slots[2, 0, device_of(i, core)] - leaves, :half]
        message[i, 3 * half + nf :] = tile[slots[2, 0, device_of(i, core ^ 1)] - leaves]
        return carry

    sends = []
    for n in range(parts):
        lax.fori_loop(n * part, (n + 1) * part, pack_rest, 0, unroll=8)
        place = pl.ds(n * part, part)
        sends.append(pltpu.make_async_copy(message.at[place], out.at[place], sems.at[n]))
        sends[n].start()
    wait_all(sends)


def top_kernel(top_list, adj, up_leaf, up_mid, couple_top, outgoing, mid_adj, own, other, total):
    rank = adj.shape[2]
    total[...] = jnp.zeros(total.shape, F32)
    for c in range(mid_adj.shape[0]):
        mid_adj[c] = lift(adj, up_leaf, c).astype(BF16)
    top_adj = lift(mid_adj, up_mid, 0).astype(BF16)
    core = lax.axis_index("grp") & 1
    for k in range(0, couple_top.shape[1], 4):
        terms = mul(top_adj, side(*[couple_top[0, k + j] for j in range(4)]))
        for j in range(4):
            p = top_list[0, k + j]
            place = ((p >> 4) & 1) ^ core
            total[place, place_of(p)] += fold(terms[:, j * rank : (j + 1) * rank])
    own[...] = total[0]
    other[...] = total[1].astype(BF16)


def start_all(copies):
    for copy in copies:
        copy.start()


def wait_all(copies):
    for copy in copies:
        copy.wait()


def adjoint_kernel(
    leaf_list_in,
    mid_list_in,
    adj_in,
    mid_adj_in,
    couple_leaf_in,
    couple_mid_in,
    out,
    other,
    leaf_pairs_out,
    mid_pairs_out,
    leaf_list,
    mid_list,
    adj,
    mid_adj,
    couple_leaf,
    couple_mid,
    leaf_pairs,
    mid_pairs,
    message,
    even,
    odd,
    sems,
    leaf_sems,
    pair_sems,
    out_sems,
):
    width, rank = couple_leaf.shape[1:3]
    nf = adj.shape[1]
    half = nf // 2
    steps = leaf_sems.shape[0]
    chunk = adj.shape[0] // steps
    is_low = lax.broadcasted_iota(jnp.int32, (half, 2 * rank), 1) < rank

    def fetch(step):
        place = pl.ds(pl.multiple_of(step * chunk, chunk), chunk)
        return pltpu.make_async_copy(couple_leaf_in.at[place], couple_leaf.at[place], leaf_sems.at[step])

    def keep_pairs(step):
        place = pl.ds(pl.multiple_of(step * chunk, chunk), chunk)
        return pltpu.make_async_copy(leaf_pairs.at[place], leaf_pairs_out.at[place], pair_sems.at[step])

    fetches = [
        pltpu.make_async_copy(leaf_list_in, leaf_list, sems.at[0]),
        pltpu.make_async_copy(mid_list_in, mid_list, sems.at[1]),
        pltpu.make_async_copy(adj_in, adj, sems.at[2]),
        pltpu.make_async_copy(mid_adj_in, mid_adj, sems.at[3]),
    ]
    fetch_mid = pltpu.make_async_copy(couple_mid_in, couple_mid, sems.at[4])
    keep_mid = pltpu.make_async_copy(mid_pairs, mid_pairs_out, sems.at[5])
    start_all(fetches)
    for step in range(steps):
        fetch(step).start()
    fetch_mid.start()

    def clear(e, carry):
        even[e] = jnp.zeros((half, 2 * rank), F32)
        odd[e] = jnp.zeros((half, 2 * rank), F32)
        return carry

    lax.fori_loop(0, even.shape[0], clear, 0, unroll=8)
    wait_all(fetches)

    def scatter(row, blocks, slot, keep):
        for k in range(0, width, 4):
            pairs = [side(blocks(k), blocks(k + 1)), side(blocks(k + 2), blocks(k + 3))]
            terms = mul(row, side(*pairs))
            for j in range(2):
                keep(k // 2 + j, pairs[j])
                pair = terms[:, 2 * j * rank : 2 * (j + 1) * rank]
                crossed = pltpu.roll(pair[half:], rank, 1)
                e, o = slot(k + 2 * j), slot(k + 2 * j + 1)
                even_sum = even[e] + jnp.where(is_low, pair[:half], crossed)
                odd_sum = odd[o] + jnp.where(is_low, crossed, pair[:half])
                even[e] = even_sum
                odd[o] = odd_sum

    def leaf_step(step, carry):
        fetch(step).wait()
        for a in range(chunk):
            g = step * chunk + a

            def keep(k, pair):
                leaf_pairs[g, k] = pair

            scatter(adj[g], lambda k: couple_leaf[g, k], lambda k: leaf_list[k, g], keep)
        keep_pairs(step).start()
        return carry

    lax.fori_loop(0, steps, leaf_step, 0)
    fetch_mid.wait()
    for c in range(mid_adj.shape[0]):

        def keep(k, pair):
            mid_pairs[c, k] = pair

        scatter(mid_adj[c], lambda k: couple_mid[c, k], lambda k: mid_list[c, k], keep)
    keep_mid.start()

    core = lax.axis_index("grp") & 1
    sends = []
    for place, target in ((1, other), (0, out)):

        def pack(i, carry):
            p = device_of(i, core ^ place)
            for s in range(3):
                e = 3 * p + s
                block = even[e] + pltpu.roll(odd[e], rank, 1)
                message[place, i, s * half : (s + 1) * half] = block.astype(BF16)
            return carry

        part = other.shape[0] // 2
        for n in range(2):
            lax.fori_loop(n * part, (n + 1) * part, pack, 0, unroll=8)
            rows = pl.ds(n * part, part)
            copy = pltpu.make_async_copy(
                message.at[place, rows], target.at[rows, pl.ds(0, 3 * half)], out_sems.at[2 * place + n]
            )
            copy.start()
            sends.append(copy)
    for step in range(steps):
        keep_pairs(step).wait()
    keep_mid.wait()
    wait_all(sends)


def gather(pairs, partner):
    near = 0
    for k in range(0, 16, 4):
        near += mul_t(side(*[partner(k + j) for j in range(4)]), side(pairs(k // 2), pairs(k // 2 + 1)))
    return near


def forward_kernel(
    leaf_list_in,
    mid_list_in,
    arrived_in,
    swapped_in,
    leaf_pairs_in,
    mid_pairs_in,
    leaf_near_out,
    mid_near_out,
    leaf_list,
    mid_list,
    arrived,
    leaf_pairs,
    mid_pairs,
    leaf_near,
    mid_near,
    coeff,
    sems,
    arrived_sems,
    leaf_sems,
    near_sems,
):
    leaves, nf, rank = leaf_near.shape
    steps = leaf_sems.shape[0]
    chunk = leaves // steps
    def leaves_of(step):
        return pl.ds(pl.multiple_of(step * chunk, chunk), chunk)

    def fetch(step):
        return pltpu.make_async_copy(leaf_pairs_in.at[leaves_of(step)], leaf_pairs.at[leaves_of(step)], leaf_sems.at[step])

    def keep(step):
        return pltpu.make_async_copy(leaf_near.at[leaves_of(step)], leaf_near_out.at[leaves_of(step)], near_sems.at[step])

    lists = [
        pltpu.make_async_copy(leaf_list_in, leaf_list, sems.at[0]),
        pltpu.make_async_copy(mid_list_in, mid_list, sems.at[1]),
    ]
    part = arrived.shape[1] // 2
    messages = []
    for n in range(2):
        rows = pl.ds(n * part, part)
        for place, source in ((0, arrived_in), (1, swapped_in)):
            piece = source.at[rows, pl.ds(0, arrived.shape[2])]
            messages.append(pltpu.make_async_copy(piece, arrived.at[place, rows], arrived_sems.at[2 * n + place]))
    fetch_mid = pltpu.make_async_copy(mid_pairs_in, mid_pairs, sems.at[2])
    keep_mid = pltpu.make_async_copy(mid_near, mid_near_out, sems.at[3])
    start_all(messages)
    start_all(lists)
    for step in range(steps):
        fetch(step).start()
    fetch_mid.start()

    core = lax.axis_index("grp") & 1

    def unpack(i, carry):
        for place in range(2):
            p = device_of(i, core ^ place)
            pair = arrived[place, i, :nf]
            coeff[3 * p] = pair[:, :rank]
            coeff[3 * p + 1] = pair[:, rank:]
            coeff[3 * p + 2] = unfold(arrived[place, i, nf:])
        return carry

    for n in range(2):
        messages[2 * n].wait()
        messages[2 * n + 1].wait()
        lax.fori_loop(n * part, (n + 1) * part, unpack, 0, unroll=4)
    wait_all(lists)

    def leaf_step(step, carry):
        fetch(step).wait()
        for a in range(chunk):
            g = step * chunk + a
            leaf_near[g] = gather(lambda k: leaf_pairs[g, k], lambda k: coeff[leaf_list[k, g]])
        keep(step).start()
        return carry

    lax.fori_loop(0, steps, leaf_step, 0)
    fetch_mid.wait()
    for c in range(mid_near.shape[0]):
        mid_near[c] = gather(lambda k: mid_pairs[c, k], lambda k: coeff[mid_list[c, k]])
    keep_mid.start()
    for step in range(steps):
        keep(step).wait()
    keep_mid.wait()


def finish_kernel(
    top_list, own_tops, other_tops, leaf_near, mid_near, up_leaf, up_mid, couple_top, forward, down_leaf, down_mid, tops
):
    rank = forward.shape[2]
    shape = (rank, rank)
    eye = (lax.broadcasted_iota(jnp.int32, shape, 0) == lax.broadcasted_iota(jnp.int32, shape, 1)).astype(BF16)
    core = lax.axis_index("grp") & 1
    tops[0] = own_tops[...]
    tops[1] = other_tops[...]

    def partner(k):
        p = top_list[0, k]
        return unfold(tops[((p >> 4) & 1) ^ core, place_of(p)])

    near = gather(lambda k: side(couple_top[0, 2 * k], couple_top[0, 2 * k + 1]), partner)
    down_mid[...] = turn(up_mid, 0, eye)
    below_top = lower(near.astype(BF16), down_mid[...])
    for c in range(mid_near.shape[0]):
        down = turn(up_leaf, c, eye)
        down_leaf[c] = down
        below = lower((mid_near[c] + below_top[c]).astype(BF16), down)
        for i in range(8):
            forward[8 * c + i] = (leaf_near[8 * c + i] + below[i]).astype(BF16)


def lower_kernel(
    slots_in,
    returned_in,
    down_leaf_in,
    down_mid_in,
    out,
    slots,
    returned,
    down_leaf,
    down_mid,
    adjoint,
    even,
    odd,
    even_mid,
    odd_mid,
    sems,
):
    leaves, nf, rank = adjoint.shape
    mids = down_leaf.shape[0]
    part = returned.shape[0] // 4
    fetches = []
    for n in range(4):
        place = pl.ds(n * part, part)
        fetches.append(pltpu.make_async_copy(returned_in.at[place], returned.at[place], sems.at[n]))
    fetch_leaf = pltpu.make_async_copy(down_leaf_in, down_leaf, sems.at[4])
    fetch_mid = pltpu.make_async_copy(down_mid_in, down_mid, sems.at[5])
    fetch_slots = pltpu.make_async_copy(slots_in, slots, sems.at[14])
    fetch_slots.start()
    start_all(fetches)
    fetch_mid.start()
    fetch_leaf.start()
    for far in (even, odd, even_mid, odd_mid):
        far[...] = jnp.zeros(far.shape, F32)
    half = nf // 2
    core = lax.axis_index("grp") & 1

    def collect(i, top):
        sums = []
        for place, far, far_mid in ((0, even, even_mid), (1, odd, odd_mid)):
            p = device_of(i, core ^ place)
            for s, held in ((0, far), (1, far), (2, far_mid)):
                u = slots[s, 0, p] - (leaves if s == 2 else 0)
                first = (3 * place + s) * half
                sums.append((held, u, held[u] + returned[i, first : first + half].astype(F32)))
        for held, u, value in sums:
            held[u] = value
        return top + returned[i, 6 * half :].astype(F32)

    fetch_slots.wait()
    top = jnp.zeros((half, 2 * rank), F32)
    for n in range(4):
        fetches[n].wait()
        top = lax.fori_loop(n * part, (n + 1) * part, collect, top, unroll=8)
    fars = [unfold(even_mid[c] + odd_mid[c]) for c in range(mids)]
    fetch_mid.wait()
    below_top = lower(unfold(top).astype(BF16), down_mid[...])
    fetch_leaf.wait()
    sends = []
    for c in range(mids):
        below = lower((fars[c] + below_top[c]).astype(BF16), down_leaf[c])
        for i in range(8):
            a = c * 8 + i
            adjoint[a] = (unfold(even[a] + odd[a]) + below[i]).astype(BF16)
        place = pl.ds(8 * c, 8)
        sends.append(pltpu.make_async_copy(adjoint.at[place], out.at[place], sems.at[6 + c]))
        sends[c].start()
    wait_all(sends)


SMEM = pl.BlockSpec(memory_space=pltpu.SMEM)
VMEM = pl.BlockSpec(memory_space=pltpu.VMEM)
HBM = pl.BlockSpec(memory_space=pl.ANY)


def exchange(x):
    order = [[device_of(i, core) for i in range(x.shape[0])] for core in range(2)]
    return lax.all_to_all(x, ("grp", "dev"), split_axis=0, concat_axis=0, axis_index_groups=order, tiled=True)


def swap(x):
    return lax.ppermute(x, "grp", [(g, g ^ 1) for g in range(lax.axis_size("grp"))])


def on_device(
    src_leaf,
    adj_leaf,
    up_leaf,
    up_mid,
    couple_leaf,
    couple_mid,
    couple_top,
    send_slots,
    leaf_list,
    mid_list,
    top_list,
):
    leaves, rank, nf = src_leaf.shape
    mids = up_mid.shape[0]
    peers = send_slots.shape[1]
    width = couple_leaf.shape[1]
    steps = mids
    src = jnp.swapaxes(src_leaf, 1, 2)
    adj = jnp.swapaxes(adj_leaf, 1, 2)
    slots = jnp.transpose(send_slots, (2, 0, 1))
    leaf_slots = leaf_list.T
    chips = peers // 2
    message = (chips, 7 * nf // 2, 2 * rank)
    swapped_message = (chips, 3 * nf // 2, 2 * rank)
    top_shape = (chips, nf // 2, 2 * rank)
    shape = jax.ShapeDtypeStruct
    params = pltpu.CompilerParams(vmem_limit_bytes=66000000)
    small = pl.CostEstimate(flops=10**6, bytes_accessed=10**5, transcendentals=0)

    outgoing = pl.pallas_call(
        lift_kernel,
        out_shape=shape(message, BF16),
        in_specs=[HBM] * 4,
        out_specs=HBM,
        scratch_shapes=[
            pltpu.SMEM(slots.shape, jnp.int32),
            pltpu.VMEM((leaves, nf, rank), BF16),
            pltpu.VMEM((leaves, rank, rank), BF16),
            pltpu.VMEM((mids, rank, rank), BF16),
            pltpu.VMEM(message, BF16),
            pltpu.VMEM((mids, nf, rank), BF16),
            pltpu.VMEM((mids, nf, 2 * rank), BF16),
            pltpu.SemaphoreType.DMA((8,)),
        ],
        compiler_params=params,
        name="lift",
    )(slots, src, up_leaf, up_mid)
    arrived = exchange(outgoing)

    mid_adj, own_terms, other_terms = pl.pallas_call(
        top_kernel,
        out_shape=(shape((mids, nf, rank), BF16), shape(top_shape, F32), shape(top_shape, BF16)),
        in_specs=[SMEM] + [VMEM] * 4 + [HBM],
        out_specs=(VMEM, VMEM, VMEM),
        scratch_shapes=[pltpu.VMEM((2,) + top_shape, F32)],
        compiler_params=params,
        cost_estimate=small,
        name="top",
    )(top_list, adj, up_leaf, up_mid, couple_top, outgoing)
    swapped_terms = swap(other_terms)
    leaf_pairs_shape = (leaves, width // 2, rank, 2 * rank)
    mid_pairs_shape = (mids, width // 2, rank, 2 * rank)
    per_slot, for_other, leaf_pairs, mid_pairs = pl.pallas_call(
        adjoint_kernel,
        out_shape=(
            shape(message, BF16),
            shape(swapped_message, BF16),
            shape(leaf_pairs_shape, BF16),
            shape(mid_pairs_shape, BF16),
        ),
        in_specs=[HBM] * 6,
        out_specs=(HBM, HBM, HBM, HBM),
        scratch_shapes=[
            pltpu.SMEM(leaf_slots.shape, jnp.int32),
            pltpu.SMEM(mid_list.shape, jnp.int32),
            pltpu.VMEM(adj.shape, BF16),
            pltpu.VMEM(mid_adj.shape, BF16),
            pltpu.VMEM(couple_leaf.shape, BF16),
            pltpu.VMEM(couple_mid.shape, BF16),
            pltpu.VMEM(leaf_pairs_shape, BF16),
            pltpu.VMEM(mid_pairs_shape, BF16),
            pltpu.VMEM((2,) + swapped_message, BF16),
            pltpu.VMEM((3 * peers, nf // 2, 2 * rank), F32),
            pltpu.VMEM((3 * peers, nf // 2, 2 * rank), F32),
            pltpu.SemaphoreType.DMA((6,)),
            pltpu.SemaphoreType.DMA((steps,)),
            pltpu.SemaphoreType.DMA((steps,)),
            pltpu.SemaphoreType.DMA((4,)),
        ],
        compiler_params=params,
        cost_estimate=small,
        name="adjoint",
    )(leaf_slots, mid_list, adj, mid_adj, couple_leaf, couple_mid)
    top_terms = (own_terms + swapped_terms.astype(F32)).astype(BF16)
    per_slot = lax.dynamic_update_slice(per_slot, swap(for_other), (0, 3 * nf // 2, 0))
    per_slot = lax.dynamic_update_slice(per_slot, top_terms, (0, 3 * nf, 0))
    returned = exchange(per_slot)

    swapped = swap(arrived[:, 3 * nf // 2 :])
    leaf_near, mid_near = pl.pallas_call(
        forward_kernel,
        out_shape=(shape((leaves, nf, rank), F32), shape((mids, nf, rank), F32)),
        in_specs=[HBM] * 6,
        out_specs=(HBM, HBM),
        scratch_shapes=[
            pltpu.SMEM(leaf_slots.shape, jnp.int32),
            pltpu.SMEM(mid_list.shape, jnp.int32),
            pltpu.VMEM((2,) + swapped_message, BF16),
            pltpu.VMEM(leaf_pairs_shape, BF16),
            pltpu.VMEM(mid_pairs_shape, BF16),
            pltpu.VMEM((leaves, nf, rank), F32),
            pltpu.VMEM((mids, nf, rank), F32),
            pltpu.VMEM((3 * peers, nf, rank), BF16),
            pltpu.SemaphoreType.DMA((4,)),
            pltpu.SemaphoreType.DMA((4,)),
            pltpu.SemaphoreType.DMA((steps,)),
            pltpu.SemaphoreType.DMA((steps,)),
        ],
        compiler_params=params,
        cost_estimate=small,
        name="forward",
    )(leaf_slots, mid_list, arrived, swapped, leaf_pairs, mid_pairs)
    forward, down_leaf, down_mid = pl.pallas_call(
        finish_kernel,
        grid=(1,),
        out_shape=(
            shape((leaves, nf, rank), BF16),
            shape((mids, rank, 8 * rank), BF16),
            shape((rank, 8 * rank), BF16),
        ),
        in_specs=[
            SMEM,
            pl.BlockSpec(top_shape, lambda _: (0, 6, 0)),
            pl.BlockSpec(top_shape, lambda _: (0, 3, 0)),
        ]
        + [VMEM] * 5,
        out_specs=(VMEM, VMEM, VMEM),
        scratch_shapes=[pltpu.VMEM((2,) + top_shape, BF16)],
        compiler_params=params,
        cost_estimate=small,
        name="finish",
    )(top_list, arrived, swapped, leaf_near, mid_near, up_leaf, up_mid, couple_top)

    adjoint = pl.pallas_call(
        lower_kernel,
        out_shape=shape((leaves, nf, rank), BF16),
        in_specs=[HBM] * 4,
        out_specs=HBM,
        scratch_shapes=[
            pltpu.SMEM(slots.shape, jnp.int32),
            pltpu.VMEM(message, BF16),
            pltpu.VMEM((mids, rank, 8 * rank), BF16),
            pltpu.VMEM((rank, 8 * rank), BF16),
            pltpu.VMEM((leaves, nf, rank), BF16),
            pltpu.VMEM((leaves, nf // 2, 2 * rank), F32),
            pltpu.VMEM((leaves, nf // 2, 2 * rank), F32),
            pltpu.VMEM((mids, nf // 2, 2 * rank), F32),
            pltpu.VMEM((mids, nf // 2, 2 * rank), F32),
            pltpu.SemaphoreType.DMA((15,)),
        ],
        compiler_params=params,
        name="lower",
    )(slots, returned, down_leaf, down_mid)
    return jnp.swapaxes(forward, 1, 2), jnp.swapaxes(adjoint, 1, 2)


def solution(mesh):
    placed = (
        P(("grp", "dev"), None, None),
        P(("grp", "dev"), None, None),
        P(("grp", "dev"), None, None),
        P(("grp", "dev"), None, None),
        P(("grp", "dev"), None, None, None),
        P(("grp", "dev"), None, None, None),
        P(("grp", "dev"), None, None, None),
        P(("grp", "dev"), None, None),
        P(("grp", "dev"), None),
        P(("grp", "dev"), None),
        P(("grp", "dev"), None),
    )
    return jax.shard_map(
        on_device,
        mesh=mesh,
        in_specs=placed,
        out_specs=(P(("grp", "dev"), None, None), P(("grp", "dev"), None, None)),
        check_vma=False,
    )
```

```python
import jax
import jax.numpy as jnp
from jax import lax
from jax.experimental import pallas as pl
from jax.experimental.pallas import tpu as pltpu
from jax.sharding import PartitionSpec as P

BF16 = jnp.bfloat16
F32 = jnp.float32


def mul(x, y):
    return lax.dot_general(x, y, (((1,), (0,)), ((), ())), preferred_element_type=F32)


def mul_t(x, y):
    return lax.dot_general(x, y, (((1,), (1,)), ((), ())), preferred_element_type=F32)


def side(*blocks):
    return jnp.concatenate(blocks, axis=1)


def fold(x):
    half = x.shape[0] // 2
    return side(x[:half], x[half:])


def unfold(x):
    half = x.shape[1] // 2
    return jnp.concatenate([x[:, :half], x[:, half:]], axis=0)


def lift(rows, up, c):
    size, rank = up.shape[1:]
    return mul(side(*[rows[8 * c + i] for i in range(8)]), up[8 * c : 8 * c + 8].reshape(8 * size, rank))


def turn(up, c, eye):
    rank, size = up.shape[1:]
    return mul_t(eye, up[8 * c : 8 * c + 8].reshape(8 * rank, size)).astype(BF16)


def lower(local, down):
    rank = down.shape[0]
    below = mul(local, down)
    return [below[:, i * rank : (i + 1) * rank] for i in range(8)]


def lift_kernel(
    slots_in, src_in, up_leaf_in, up_mid_in, out, slots, src, up_leaf, up_mid, message, mid_src, tile, sems
):
    leaves, nf, rank = src.shape
    mids = up_mid.shape[0]
    parts = 4
    part = out.shape[0] // parts
    fetch_src = pltpu.make_async_copy(src_in, src, sems.at[4])
    fetch_leaf = pltpu.make_async_copy(up_leaf_in, up_leaf, sems.at[5])
    fetch_mid = pltpu.make_async_copy(up_mid_in, up_mid, sems.at[6])
    fetch_slots = pltpu.make_async_copy(slots_in, slots, sems.at[7])
    fetch_slots.start()
    fetch_src.start()
    fetch_leaf.start()
    fetch_mid.start()

    def pack_leaf(p, carry):
        message[p, :nf] = side(src[slots[0, 0, p]], src[slots[1, 0, p]])
        return carry

    fetch_slots.wait()
    fetch_src.wait()
    lax.fori_loop(0, out.shape[0], pack_leaf, 0, unroll=16)
    fetch_leaf.wait()
    for c in range(mids):
        mid_src[c] = lift(src, up_leaf, c).astype(BF16)
    fetch_mid.wait()
    top_src = lift(mid_src, up_mid, 0).astype(BF16)
    for core in range(2):
        top_half = fold(top_src[core * nf // 2 : (core + 1) * nf // 2])
        for c in range(mids):
            tile[core, c] = jnp.concatenate([fold(mid_src[c]), top_half], axis=0)

    sends = []
    for n in range(parts):
        for core in range(2):

            def pack_rest(i, carry):
                p = n * part + core * (part // 2) + i
                message[p, nf:] = tile[core, slots[2, 0, p] - leaves]
                return carry

            lax.fori_loop(0, part // 2, pack_rest, 0, unroll=16)
        place = pl.ds(n * part, part)
        sends.append(pltpu.make_async_copy(message.at[place], out.at[place], sems.at[n]))
        sends[n].start()
    wait_all(sends)


def device_of(i, core):
    return (i >> 4) * 32 + core * 16 + (i & 15)


def place_of(p):
    return (p >> 5) * 16 + (p & 15)


def top_kernel(top_list, adj, up_leaf, up_mid, couple_top, outgoing, mid_adj, own, other, total):
    rank = adj.shape[2]
    total[...] = jnp.zeros(total.shape, F32)
    for c in range(mid_adj.shape[0]):
        mid_adj[c] = lift(adj, up_leaf, c).astype(BF16)
    top_adj = lift(mid_adj, up_mid, 0).astype(BF16)
    core = lax.axis_index("grp") & 1
    for k in range(0, couple_top.shape[1], 4):
        terms = mul(top_adj, side(*[couple_top[0, k + j] for j in range(4)]))
        for j in range(4):
            p = top_list[0, k + j]
            place = ((p >> 4) & 1) ^ core
            total[place, place_of(p)] += fold(terms[:, j * rank : (j + 1) * rank])
    own[...] = total[0]
    other[...] = total[1].astype(BF16)


def start_all(copies):
    for copy in copies:
        copy.start()


def wait_all(copies):
    for copy in copies:
        copy.wait()


def adjoint_kernel(
    leaf_list_in,
    mid_list_in,
    adj_in,
    mid_adj_in,
    couple_leaf_in,
    couple_mid_in,
    out,
    other,
    leaf_pairs_out,
    mid_pairs_out,
    leaf_list,
    mid_list,
    adj,
    mid_adj,
    couple_leaf,
    couple_mid,
    leaf_pairs,
    mid_pairs,
    message,
    even,
    odd,
    sems,
    leaf_sems,
    pair_sems,
    out_sems,
):
    width, rank = couple_leaf.shape[1:3]
    nf = adj.shape[1]
    half = nf // 2
    steps = leaf_sems.shape[0]
    chunk = adj.shape[0] // steps
    is_low = lax.broadcasted_iota(jnp.int32, (half, 2 * rank), 1) < rank

    def fetch(step):
        place = pl.ds(pl.multiple_of(step * chunk, chunk), chunk)
        return pltpu.make_async_copy(couple_leaf_in.at[place], couple_leaf.at[place], leaf_sems.at[step])

    def keep_pairs(step):
        place = pl.ds(pl.multiple_of(step * chunk, chunk), chunk)
        return pltpu.make_async_copy(leaf_pairs.at[place], leaf_pairs_out.at[place], pair_sems.at[step])

    fetches = [
        pltpu.make_async_copy(leaf_list_in, leaf_list, sems.at[0]),
        pltpu.make_async_copy(mid_list_in, mid_list, sems.at[1]),
        pltpu.make_async_copy(adj_in, adj, sems.at[2]),
        pltpu.make_async_copy(mid_adj_in, mid_adj, sems.at[3]),
    ]
    fetch_mid = pltpu.make_async_copy(couple_mid_in, couple_mid, sems.at[4])
    keep_mid = pltpu.make_async_copy(mid_pairs, mid_pairs_out, sems.at[5])
    start_all(fetches)
    for step in range(steps):
        fetch(step).start()
    fetch_mid.start()

    def clear(e, carry):
        even[e] = jnp.zeros((half, 2 * rank), F32)
        odd[e] = jnp.zeros((half, 2 * rank), F32)
        return carry

    lax.fori_loop(0, even.shape[0], clear, 0, unroll=8)
    wait_all(fetches)

    def scatter(row, blocks, slot, keep):
        for k in range(0, width, 4):
            pairs = [side(blocks(k), blocks(k + 1)), side(blocks(k + 2), blocks(k + 3))]
            terms = mul(row, side(*pairs))
            for j in range(2):
                keep(k // 2 + j, pairs[j])
                pair = terms[:, 2 * j * rank : 2 * (j + 1) * rank]
                crossed = pltpu.roll(pair[half:], rank, 1)
                e, o = slot(k + 2 * j), slot(k + 2 * j + 1)
                even_sum = even[e] + jnp.where(is_low, pair[:half], crossed)
                odd_sum = odd[o] + jnp.where(is_low, crossed, pair[:half])
                even[e] = even_sum
                odd[o] = odd_sum

    def leaf_step(step, carry):
        fetch(step).wait()
        for a in range(chunk):
            g = step * chunk + a

            def keep(k, pair):
                leaf_pairs[g, k] = pair

            scatter(adj[g], lambda k: couple_leaf[g, k], lambda k: leaf_list[k, g], keep)
        keep_pairs(step).start()
        return carry

    lax.fori_loop(0, steps, leaf_step, 0)
    fetch_mid.wait()
    for c in range(mid_adj.shape[0]):

        def keep(k, pair):
            mid_pairs[c, k] = pair

        scatter(mid_adj[c], lambda k: couple_mid[c, k], lambda k: mid_list[c, k], keep)
    keep_mid.start()

    core = lax.axis_index("grp") & 1
    sends = []
    for place, target in ((1, other), (0, out)):

        def pack(i, carry):
            p = device_of(i, core ^ place)
            for s in range(3):
                e = 3 * p + s
                block = even[e] + pltpu.roll(odd[e], rank, 1)
                message[place, i, s * half : (s + 1) * half] = block.astype(BF16)
            return carry

        part = other.shape[0] // 2
        for n in range(2):
            lax.fori_loop(n * part, (n + 1) * part, pack, 0, unroll=8)
            rows = pl.ds(n * part, part)
            copy = pltpu.make_async_copy(
                message.at[place, rows], target.at[rows, pl.ds(0, 3 * half)], out_sems.at[2 * place + n]
            )
            copy.start()
            sends.append(copy)
    for step in range(steps):
        keep_pairs(step).wait()
    keep_mid.wait()
    wait_all(sends)


def gather(pairs, partner):
    near = 0
    for k in range(0, 16, 4):
        near += mul_t(side(*[partner(k + j) for j in range(4)]), side(pairs(k // 2), pairs(k // 2 + 1)))
    return near


def forward_kernel(
    leaf_list_in,
    mid_list_in,
    arrived_in,
    leaf_pairs_in,
    mid_pairs_in,
    leaf_near_out,
    mid_near_out,
    leaf_list,
    mid_list,
    arrived,
    leaf_pairs,
    mid_pairs,
    leaf_near,
    mid_near,
    coeff,
    sems,
    arrived_sems,
    leaf_sems,
    near_sems,
):
    leaves, nf, rank = leaf_near.shape
    steps = leaf_sems.shape[0]
    chunk = leaves // steps
    parts = arrived_sems.shape[0]
    part = arrived.shape[0] // parts

    def place(step):
        return pl.ds(pl.multiple_of(step * chunk, chunk), chunk)

    def fetch(step):
        return pltpu.make_async_copy(leaf_pairs_in.at[place(step)], leaf_pairs.at[place(step)], leaf_sems.at[step])

    def keep(step):
        return pltpu.make_async_copy(leaf_near.at[place(step)], leaf_near_out.at[place(step)], near_sems.at[step])

    lists = [
        pltpu.make_async_copy(leaf_list_in, leaf_list, sems.at[0]),
        pltpu.make_async_copy(mid_list_in, mid_list, sems.at[1]),
    ]
    messages = []
    for n in range(parts):
        rows_n = pl.ds(n * part, part)
        messages.append(pltpu.make_async_copy(arrived_in.at[rows_n], arrived.at[rows_n], arrived_sems.at[n]))
    fetch_mid = pltpu.make_async_copy(mid_pairs_in, mid_pairs, sems.at[2])
    keep_mid = pltpu.make_async_copy(mid_near, mid_near_out, sems.at[3])
    start_all(messages)
    start_all(lists)
    for step in range(steps):
        fetch(step).start()
    fetch_mid.start()

    def unpack(p, carry):
        pair = arrived[p, :nf]
        coeff[3 * p] = pair[:, :rank]
        coeff[3 * p + 1] = pair[:, rank:]
        coeff[3 * p + 2] = unfold(arrived[p, nf : nf + nf // 2])
        return carry

    for n in range(parts):
        messages[n].wait()
        lax.fori_loop(n * part, (n + 1) * part, unpack, 0, unroll=8)
    wait_all(lists)

    def leaf_step(step, carry):
        fetch(step).wait()
        for a in range(chunk):
            g = step * chunk + a
            leaf_near[g] = gather(lambda k: leaf_pairs[g, k], lambda k: coeff[leaf_list[k, g]])
        keep(step).start()
        return carry

    lax.fori_loop(0, steps, leaf_step, 0)
    fetch_mid.wait()
    for c in range(mid_near.shape[0]):
        mid_near[c] = gather(lambda k: mid_pairs[c, k], lambda k: coeff[mid_list[c, k]])
    keep_mid.start()
    for step in range(steps):
        keep(step).wait()
    keep_mid.wait()


def finish_kernel(
    top_list, own_half, other_half, leaf_near, mid_near, up_leaf, up_mid, couple_top, forward, down_leaf, down_mid
):
    nf, rank = forward.shape[1:]
    shape = (rank, rank)
    eye = (lax.broadcasted_iota(jnp.int32, shape, 0) == lax.broadcasted_iota(jnp.int32, shape, 1)).astype(BF16)

    def partner(k):
        j = top_list[0, k]
        return jnp.concatenate([unfold(own_half[j]), unfold(other_half[j])], axis=0)

    near = gather(lambda k: side(couple_top[0, 2 * k], couple_top[0, 2 * k + 1]), partner)
    swapped = jnp.concatenate([near[nf // 2 :], near[: nf // 2]], axis=0)
    core = lax.axis_index("grp") % 2
    down_mid[...] = turn(up_mid, 0, eye)
    below_top = lower(jnp.where(core == 0, near, swapped).astype(BF16), down_mid[...])
    for c in range(mid_near.shape[0]):
        down = turn(up_leaf, c, eye)
        down_leaf[c] = down
        below = lower((mid_near[c] + below_top[c]).astype(BF16), down)
        for i in range(8):
            forward[8 * c + i] = (leaf_near[8 * c + i] + below[i]).astype(BF16)


def lower_kernel(slots, returned, down_leaf, down_mid, out, adjoint, even, odd, even_mid, odd_mid, sems):
    leaves, nf, rank = adjoint.shape
    mids = down_leaf.shape[0]
    for far in (even, odd, even_mid, odd_mid):
        far[...] = jnp.zeros(far.shape, F32)
    half = nf // 2
    core = lax.axis_index("grp") & 1

    def collect(i, top):
        sums = []
        for place, far, far_mid in ((0, even, even_mid), (1, odd, odd_mid)):
            p = device_of(i, core ^ place)
            for s, held in ((0, far), (1, far), (2, far_mid)):
                u = slots[s, 0, p] - (leaves if s == 2 else 0)
                first = (3 * place + s) * half
                sums.append((held, u, held[u] + returned[i, first : first + half].astype(F32)))
        for held, u, value in sums:
            held[u] = value
        return top + returned[i, 6 * half :].astype(F32)

    top = lax.fori_loop(0, returned.shape[0], collect, jnp.zeros((half, 2 * rank), F32), unroll=8)
    fars = [unfold(even_mid[c] + odd_mid[c]) for c in range(mids)]
    below_top = lower(unfold(top).astype(BF16), down_mid[...])
    sends = []
    for c in range(mids):
        below = lower((fars[c] + below_top[c]).astype(BF16), down_leaf[c])
        for i in range(8):
            a = c * 8 + i
            adjoint[a] = (unfold(even[a] + odd[a]) + below[i]).astype(BF16)
        place = pl.ds(8 * c, 8)
        sends.append(pltpu.make_async_copy(adjoint.at[place], out.at[place], sems.at[c]))
        sends[c].start()
    wait_all(sends)


SMEM = pl.BlockSpec(memory_space=pltpu.SMEM)
VMEM = pl.BlockSpec(memory_space=pltpu.VMEM)
HBM = pl.BlockSpec(memory_space=pl.ANY)


def exchange(x):
    return lax.all_to_all(x, ("grp", "dev"), split_axis=0, concat_axis=0, tiled=True)


def swap(x):
    return lax.ppermute(x, "grp", [(g, g ^ 1) for g in range(lax.axis_size("grp"))])


def on_device(
    src_leaf,
    adj_leaf,
    up_leaf,
    up_mid,
    couple_leaf,
    couple_mid,
    couple_top,
    send_slots,
    leaf_list,
    mid_list,
    top_list,
):
    leaves, rank, nf = src_leaf.shape
    mids = up_mid.shape[0]
    peers = send_slots.shape[1]
    width = couple_leaf.shape[1]
    steps = mids
    src = jnp.swapaxes(src_leaf, 1, 2)
    adj = jnp.swapaxes(adj_leaf, 1, 2)
    slots = jnp.transpose(send_slots, (2, 0, 1))
    leaf_slots = leaf_list.T
    message = (peers, 7 * nf // 4, 2 * rank)
    chips = peers // 2
    second_message = (chips, 7 * nf // 2, 2 * rank)
    swapped_message = (chips, 3 * nf // 2, 2 * rank)
    top_shape = (chips, nf // 2, 2 * rank)
    shape = jax.ShapeDtypeStruct
    params = pltpu.CompilerParams(vmem_limit_bytes=66000000)
    roomy = pltpu.CompilerParams(vmem_limit_bytes=64000000)
    small = pl.CostEstimate(flops=10**6, bytes_accessed=10**5, transcendentals=0)

    outgoing = pl.pallas_call(
        lift_kernel,
        out_shape=shape(message, BF16),
        in_specs=[HBM] * 4,
        out_specs=HBM,
        scratch_shapes=[
            pltpu.SMEM(slots.shape, jnp.int32),
            pltpu.VMEM((leaves, nf, rank), BF16),
            pltpu.VMEM((leaves, rank, rank), BF16),
            pltpu.VMEM((mids, rank, rank), BF16),
            pltpu.VMEM(message, BF16),
            pltpu.VMEM((mids, nf, rank), BF16),
            pltpu.VMEM((2, mids, 3 * nf // 4, 2 * rank), BF16),
            pltpu.SemaphoreType.DMA((8,)),
        ],
        compiler_params=params,
        name="lift",
    )(slots, src, up_leaf, up_mid)
    arrived = exchange(outgoing)

    mid_adj, own_terms, other_terms = pl.pallas_call(
        top_kernel,
        out_shape=(shape((mids, nf, rank), BF16), shape(top_shape, F32), shape(top_shape, BF16)),
        in_specs=[SMEM] + [VMEM] * 4 + [HBM],
        out_specs=(VMEM, VMEM, VMEM),
        scratch_shapes=[pltpu.VMEM((2,) + top_shape, F32)],
        compiler_params=params,
        cost_estimate=small,
        name="top",
    )(top_list, adj, up_leaf, up_mid, couple_top, outgoing)
    swapped_terms = swap(other_terms)
    leaf_pairs_shape = (leaves, width // 2, rank, 2 * rank)
    mid_pairs_shape = (mids, width // 2, rank, 2 * rank)
    per_slot, for_other, leaf_pairs, mid_pairs = pl.pallas_call(
        adjoint_kernel,
        out_shape=(
            shape(second_message, BF16),
            shape(swapped_message, BF16),
            shape(leaf_pairs_shape, BF16),
            shape(mid_pairs_shape, BF16),
        ),
        in_specs=[HBM] * 6,
        out_specs=(HBM, HBM, HBM, HBM),
        scratch_shapes=[
            pltpu.SMEM(leaf_slots.shape, jnp.int32),
            pltpu.SMEM(mid_list.shape, jnp.int32),
            pltpu.VMEM(adj.shape, BF16),
            pltpu.VMEM(mid_adj.shape, BF16),
            pltpu.VMEM(couple_leaf.shape, BF16),
            pltpu.VMEM(couple_mid.shape, BF16),
            pltpu.VMEM(leaf_pairs_shape, BF16),
            pltpu.VMEM(mid_pairs_shape, BF16),
            pltpu.VMEM((2,) + swapped_message, BF16),
            pltpu.VMEM((3 * peers, nf // 2, 2 * rank), F32),
            pltpu.VMEM((3 * peers, nf // 2, 2 * rank), F32),
            pltpu.SemaphoreType.DMA((6,)),
            pltpu.SemaphoreType.DMA((steps,)),
            pltpu.SemaphoreType.DMA((steps,)),
            pltpu.SemaphoreType.DMA((4,)),
        ],
        compiler_params=params,
        cost_estimate=small,
        name="adjoint",
    )(leaf_slots, mid_list, adj, mid_adj, couple_leaf, couple_mid)
    top_terms = (own_terms + swapped_terms.astype(F32)).astype(BF16)
    per_slot = lax.dynamic_update_slice(per_slot, swap(for_other), (0, 3 * nf // 2, 0))
    per_slot = lax.dynamic_update_slice(per_slot, top_terms, (0, 3 * nf, 0))
    same_core = [[device_of(i, core) for i in range(chips)] for core in range(2)]
    returned = lax.all_to_all(
        per_slot, ("grp", "dev"), split_axis=0, concat_axis=0, axis_index_groups=same_core, tiled=True
    )

    own_half = arrived[:, 3 * nf // 2 :]
    other_half = swap(own_half)
    leaf_near, mid_near = pl.pallas_call(
        forward_kernel,
        out_shape=(shape((leaves, nf, rank), F32), shape((mids, nf, rank), F32)),
        in_specs=[HBM] * 5,
        out_specs=(HBM, HBM),
        scratch_shapes=[
            pltpu.SMEM(leaf_slots.shape, jnp.int32),
            pltpu.SMEM(mid_list.shape, jnp.int32),
            pltpu.VMEM(message, BF16),
            pltpu.VMEM(leaf_pairs_shape, BF16),
            pltpu.VMEM(mid_pairs_shape, BF16),
            pltpu.VMEM((leaves, nf, rank), F32),
            pltpu.VMEM((mids, nf, rank), F32),
            pltpu.VMEM((3 * peers, nf, rank), BF16),
            pltpu.SemaphoreType.DMA((4,)),
            pltpu.SemaphoreType.DMA((4,)),
            pltpu.SemaphoreType.DMA((steps,)),
            pltpu.SemaphoreType.DMA((steps,)),
        ],
        compiler_params=roomy,
        cost_estimate=small,
        name="forward",
    )(leaf_slots, mid_list, arrived, leaf_pairs, mid_pairs)
    forward, down_leaf, down_mid = pl.pallas_call(
        finish_kernel,
        out_shape=(
            shape((leaves, nf, rank), BF16),
            shape((mids, rank, 8 * rank), BF16),
            shape((rank, 8 * rank), BF16),
        ),
        in_specs=[SMEM] + [VMEM] * 7,
        out_specs=(VMEM, VMEM, VMEM),
        compiler_params=roomy,
        cost_estimate=small,
        name="finish",
    )(top_list, own_half, other_half, leaf_near, mid_near, up_leaf, up_mid, couple_top)

    adjoint = pl.pallas_call(
        lower_kernel,
        out_shape=shape((leaves, nf, rank), BF16),
        in_specs=[SMEM, VMEM, VMEM, VMEM],
        out_specs=HBM,
        scratch_shapes=[
            pltpu.VMEM((leaves, nf, rank), BF16),
            pltpu.VMEM((leaves, nf // 2, 2 * rank), F32),
            pltpu.VMEM((leaves, nf // 2, 2 * rank), F32),
            pltpu.VMEM((mids, nf // 2, 2 * rank), F32),
            pltpu.VMEM((mids, nf // 2, 2 * rank), F32),
            pltpu.SemaphoreType.DMA((mids,)),
        ],
        compiler_params=pltpu.CompilerParams(vmem_limit_bytes=40000000),
        name="lower",
    )(slots, returned, down_leaf, down_mid)
    return jnp.swapaxes(forward, 1, 2), jnp.swapaxes(adjoint, 1, 2)


def solution(mesh):
    placed = (
        P(("grp", "dev"), None, None),
        P(("grp", "dev"), None, None),
        P(("grp", "dev"), None, None),
        P(("grp", "dev"), None, None),
        P(("grp", "dev"), None, None, None),
        P(("grp", "dev"), None, None, None),
        P(("grp", "dev"), None, None, None),
        P(("grp", "dev"), None, None),
        P(("grp", "dev"), None),
        P(("grp", "dev"), None),
        P(("grp", "dev"), None),
    )
    return jax.shard_map(
        on_device,
        mesh=mesh,
        in_specs=placed,
        out_specs=(P(("grp", "dev"), None, None), P(("grp", "dev"), None, None)),
        check_vma=False,
    )
```

```python
import jax
import jax.numpy as jnp
from jax import lax
from jax.experimental import pallas as pl
from jax.experimental.pallas import tpu as pltpu
from jax.sharding import PartitionSpec as P

BF16 = jnp.bfloat16
F32 = jnp.float32


def mul(x, y):
    return lax.dot_general(x, y, (((1,), (0,)), ((), ())), preferred_element_type=F32)


def mul_t(x, y):
    return lax.dot_general(x, y, (((1,), (1,)), ((), ())), preferred_element_type=F32)


def side(*blocks):
    return jnp.concatenate(blocks, axis=1)


def fold(x):
    half = x.shape[0] // 2
    return side(x[:half], x[half:])


def unfold(x):
    half = x.shape[1] // 2
    return jnp.concatenate([x[:, :half], x[:, half:]], axis=0)


def lift(rows, up, c):
    size, rank = up.shape[1:]
    return mul(side(*[rows[8 * c + i] for i in range(8)]), up[8 * c : 8 * c + 8].reshape(8 * size, rank))


def turn(up, c, eye):
    rank, size = up.shape[1:]
    return mul_t(eye, up[8 * c : 8 * c + 8].reshape(8 * rank, size)).astype(BF16)


def lower(local, down):
    rank = down.shape[0]
    below = mul(local, down)
    return [below[:, i * rank : (i + 1) * rank] for i in range(8)]


def lift_kernel(
    slots_in, src_in, up_leaf_in, up_mid_in, out, slots, src, up_leaf, up_mid, message, mid_src, tile, sems
):
    leaves, nf, rank = src.shape
    mids = up_mid.shape[0]
    parts = 4
    part = out.shape[0] // parts
    fetch_src = pltpu.make_async_copy(src_in, src, sems.at[4])
    fetch_leaf = pltpu.make_async_copy(up_leaf_in, up_leaf, sems.at[5])
    fetch_mid = pltpu.make_async_copy(up_mid_in, up_mid, sems.at[6])
    fetch_slots = pltpu.make_async_copy(slots_in, slots, sems.at[7])
    fetch_slots.start()
    fetch_src.start()
    fetch_leaf.start()
    fetch_mid.start()

    def pack_leaf(p, carry):
        message[p, :nf] = side(src[slots[0, 0, p]], src[slots[1, 0, p]])
        return carry

    fetch_slots.wait()
    fetch_src.wait()
    lax.fori_loop(0, out.shape[0], pack_leaf, 0, unroll=16)
    fetch_leaf.wait()
    for c in range(mids):
        mid_src[c] = lift(src, up_leaf, c).astype(BF16)
    fetch_mid.wait()
    top_src = lift(mid_src, up_mid, 0).astype(BF16)
    for core in range(2):
        top_half = fold(top_src[core * nf // 2 : (core + 1) * nf // 2])
        for c in range(mids):
            tile[core, c] = jnp.concatenate([fold(mid_src[c]), top_half], axis=0)

    sends = []
    for n in range(parts):
        for core in range(2):

            def pack_rest(i, carry):
                p = n * part + core * (part // 2) + i
                message[p, nf:] = tile[core, slots[2, 0, p] - leaves]
                return carry

            lax.fori_loop(0, part // 2, pack_rest, 0, unroll=16)
        place = pl.ds(n * part, part)
        sends.append(pltpu.make_async_copy(message.at[place], out.at[place], sems.at[n]))
        sends[n].start()
    wait_all(sends)


def device_of(i, core):
    return (i >> 4) * 32 + core * 16 + (i & 15)


def place_of(p):
    return (p >> 5) * 16 + (p & 15)


def top_kernel(top_list, adj, up_leaf, up_mid, couple_top, outgoing, mid_adj, own, other, total):
    rank = adj.shape[2]
    total[...] = jnp.zeros(total.shape, F32)
    for c in range(mid_adj.shape[0]):
        mid_adj[c] = lift(adj, up_leaf, c).astype(BF16)
    top_adj = lift(mid_adj, up_mid, 0).astype(BF16)
    core = lax.axis_index("grp") & 1
    for k in range(0, couple_top.shape[1], 4):
        terms = mul(top_adj, side(*[couple_top[0, k + j] for j in range(4)]))
        for j in range(4):
            p = top_list[0, k + j]
            place = ((p >> 4) & 1) ^ core
            total[place, place_of(p)] += fold(terms[:, j * rank : (j + 1) * rank])
    own[...] = total[0]
    other[...] = total[1].astype(BF16)


def start_all(copies):
    for copy in copies:
        copy.start()


def wait_all(copies):
    for copy in copies:
        copy.wait()


def adjoint_kernel(
    leaf_list_in,
    mid_list_in,
    adj_in,
    mid_adj_in,
    couple_leaf_in,
    couple_mid_in,
    out,
    other,
    leaf_pairs_out,
    mid_pairs_out,
    leaf_list,
    mid_list,
    adj,
    mid_adj,
    couple_leaf,
    couple_mid,
    leaf_pairs,
    mid_pairs,
    message,
    even,
    odd,
    sems,
    leaf_sems,
    pair_sems,
    out_sems,
):
    width, rank = couple_leaf.shape[1:3]
    nf = adj.shape[1]
    half = nf // 2
    steps = leaf_sems.shape[0]
    chunk = adj.shape[0] // steps
    is_low = lax.broadcasted_iota(jnp.int32, (half, 2 * rank), 1) < rank

    def fetch(step):
        place = pl.ds(pl.multiple_of(step * chunk, chunk), chunk)
        return pltpu.make_async_copy(couple_leaf_in.at[place], couple_leaf.at[place], leaf_sems.at[step])

    def keep_pairs(step):
        place = pl.ds(pl.multiple_of(step * chunk, chunk), chunk)
        return pltpu.make_async_copy(leaf_pairs.at[place], leaf_pairs_out.at[place], pair_sems.at[step])

    fetches = [
        pltpu.make_async_copy(leaf_list_in, leaf_list, sems.at[0]),
        pltpu.make_async_copy(mid_list_in, mid_list, sems.at[1]),
        pltpu.make_async_copy(adj_in, adj, sems.at[2]),
        pltpu.make_async_copy(mid_adj_in, mid_adj, sems.at[3]),
    ]
    fetch_mid = pltpu.make_async_copy(couple_mid_in, couple_mid, sems.at[4])
    keep_mid = pltpu.make_async_copy(mid_pairs, mid_pairs_out, sems.at[5])
    start_all(fetches)
    for step in range(steps):
        fetch(step).start()
    fetch_mid.start()

    def clear(e, carry):
        even[e] = jnp.zeros((half, 2 * rank), F32)
        odd[e] = jnp.zeros((half, 2 * rank), F32)
        return carry

    lax.fori_loop(0, even.shape[0], clear, 0, unroll=8)
    wait_all(fetches)

    def scatter(row, blocks, slot, keep):
        for k in range(0, width, 4):
            pairs = [side(blocks(k), blocks(k + 1)), side(blocks(k + 2), blocks(k + 3))]
            terms = mul(row, side(*pairs))
            for j in range(2):
                keep(k // 2 + j, pairs[j])
                pair = terms[:, 2 * j * rank : 2 * (j + 1) * rank]
                crossed = pltpu.roll(pair[half:], rank, 1)
                e, o = slot(k + 2 * j), slot(k + 2 * j + 1)
                even_sum = even[e] + jnp.where(is_low, pair[:half], crossed)
                odd_sum = odd[o] + jnp.where(is_low, crossed, pair[:half])
                even[e] = even_sum
                odd[o] = odd_sum

    def leaf_step(step, carry):
        fetch(step).wait()
        for a in range(chunk):
            g = step * chunk + a

            def keep(k, pair):
                leaf_pairs[g, k] = pair

            scatter(adj[g], lambda k: couple_leaf[g, k], lambda k: leaf_list[k, g], keep)
        keep_pairs(step).start()
        return carry

    lax.fori_loop(0, steps, leaf_step, 0)
    fetch_mid.wait()
    for c in range(mid_adj.shape[0]):

        def keep(k, pair):
            mid_pairs[c, k] = pair

        scatter(mid_adj[c], lambda k: couple_mid[c, k], lambda k: mid_list[c, k], keep)
    keep_mid.start()

    core = lax.axis_index("grp") & 1
    sends = []
    for place, target in ((1, other), (0, out)):

        def pack(i, carry):
            p = device_of(i, core ^ place)
            for s in range(3):
                e = 3 * p + s
                block = even[e] + pltpu.roll(odd[e], rank, 1)
                message[place, i, s * half : (s + 1) * half] = block.astype(BF16)
            return carry

        part = other.shape[0] // 2
        for n in range(2):
            lax.fori_loop(n * part, (n + 1) * part, pack, 0, unroll=8)
            rows = pl.ds(n * part, part)
            copy = pltpu.make_async_copy(
                message.at[place, rows], target.at[rows, pl.ds(0, 3 * half)], out_sems.at[2 * place + n]
            )
            copy.start()
            sends.append(copy)
    for step in range(steps):
        keep_pairs(step).wait()
    keep_mid.wait()
    wait_all(sends)


def gather(pairs, partner):
    near = 0
    for k in range(0, 16, 4):
        near += mul_t(side(*[partner(k + j) for j in range(4)]), side(pairs(k // 2), pairs(k // 2 + 1)))
    return near


def forward_kernel(
    leaf_list_in,
    mid_list_in,
    arrived_in,
    leaf_pairs_in,
    mid_pairs_in,
    leaf_near_out,
    mid_near_out,
    leaf_list,
    mid_list,
    arrived,
    leaf_pairs,
    mid_pairs,
    leaf_near,
    mid_near,
    coeff,
    sems,
    arrived_sems,
    leaf_sems,
    near_sems,
):
    leaves, nf, rank = leaf_near.shape
    steps = leaf_sems.shape[0]
    chunk = leaves // steps
    parts = arrived_sems.shape[0]
    part = arrived.shape[0] // parts

    def place(step):
        return pl.ds(pl.multiple_of(step * chunk, chunk), chunk)

    def fetch(step):
        return pltpu.make_async_copy(leaf_pairs_in.at[place(step)], leaf_pairs.at[place(step)], leaf_sems.at[step])

    def keep(step):
        return pltpu.make_async_copy(leaf_near.at[place(step)], leaf_near_out.at[place(step)], near_sems.at[step])

    lists = [
        pltpu.make_async_copy(leaf_list_in, leaf_list, sems.at[0]),
        pltpu.make_async_copy(mid_list_in, mid_list, sems.at[1]),
    ]
    messages = []
    for n in range(parts):
        rows_n = pl.ds(n * part, part)
        messages.append(pltpu.make_async_copy(arrived_in.at[rows_n], arrived.at[rows_n], arrived_sems.at[n]))
    fetch_mid = pltpu.make_async_copy(mid_pairs_in, mid_pairs, sems.at[2])
    keep_mid = pltpu.make_async_copy(mid_near, mid_near_out, sems.at[3])
    start_all(messages)
    start_all(lists)
    for step in range(steps):
        fetch(step).start()
    fetch_mid.start()

    def unpack(p, carry):
        pair = arrived[p, :nf]
        coeff[3 * p] = pair[:, :rank]
        coeff[3 * p + 1] = pair[:, rank:]
        coeff[3 * p + 2] = unfold(arrived[p, nf : nf + nf // 2])
        return carry

    for n in range(parts):
        messages[n].wait()
        lax.fori_loop(n * part, (n + 1) * part, unpack, 0, unroll=8)
    wait_all(lists)

    def leaf_step(step, carry):
        fetch(step).wait()
        for a in range(chunk):
            g = step * chunk + a
            leaf_near[g] = gather(lambda k: leaf_pairs[g, k], lambda k: coeff[leaf_list[k, g]])
        keep(step).start()
        return carry

    lax.fori_loop(0, steps, leaf_step, 0)
    fetch_mid.wait()
    for c in range(mid_near.shape[0]):
        mid_near[c] = gather(lambda k: mid_pairs[c, k], lambda k: coeff[mid_list[c, k]])
    keep_mid.start()
    for step in range(steps):
        keep(step).wait()
    keep_mid.wait()


def finish_kernel(
    top_list, own_half, other_half, leaf_near, mid_near, up_leaf, up_mid, couple_top, forward, down_all
):
    nf, rank = forward.shape[1:]
    shape = (rank, rank)
    eye = (lax.broadcasted_iota(jnp.int32, shape, 0) == lax.broadcasted_iota(jnp.int32, shape, 1)).astype(BF16)

    def partner(k):
        j = top_list[0, k]
        return jnp.concatenate([unfold(own_half[j]), unfold(other_half[j])], axis=0)

    near = gather(lambda k: side(couple_top[0, 2 * k], couple_top[0, 2 * k + 1]), partner)
    swapped = jnp.concatenate([near[nf // 2 :], near[: nf // 2]], axis=0)
    core = lax.axis_index("grp") % 2
    mids = mid_near.shape[0]
    down_all[mids] = turn(up_mid, 0, eye)
    below_top = lower(jnp.where(core == 0, near, swapped).astype(BF16), down_all[mids])
    for c in range(mids):
        down = turn(up_leaf, c, eye)
        down_all[c] = down
        below = lower((mid_near[c] + below_top[c]).astype(BF16), down)
        for i in range(8):
            forward[8 * c + i] = (leaf_near[8 * c + i] + below[i]).astype(BF16)


def lower_kernel(
    slots, returned, down_all_in, out, down_all, adjoint, even, odd, even_mid, odd_mid, sems
):
    leaves, nf, rank = adjoint.shape
    mids = even_mid.shape[0]
    fetch = pltpu.make_async_copy(down_all_in, down_all, sems.at[mids])
    fetch.start()
    for far in (even, odd, even_mid, odd_mid):
        far[...] = jnp.zeros(far.shape, F32)
    half = nf // 2
    core = lax.axis_index("grp") & 1

    def collect(i, top):
        sums = []
        for place, far, far_mid in ((0, even, even_mid), (1, odd, odd_mid)):
            p = device_of(i, core ^ place)
            for s, held in ((0, far), (1, far), (2, far_mid)):
                u = slots[s, 0, p] - (leaves if s == 2 else 0)
                first = (3 * place + s) * half
                sums.append((held, u, held[u] + returned[i, first : first + half].astype(F32)))
        for held, u, value in sums:
            held[u] = value
        return top + returned[i, 6 * half :].astype(F32)

    top = lax.fori_loop(0, returned.shape[0], collect, jnp.zeros((half, 2 * rank), F32), unroll=8)
    fars = [unfold(even_mid[c] + odd_mid[c]) for c in range(mids)]
    fetch.wait()
    below_top = lower(unfold(top).astype(BF16), down_all[mids])
    sends = []
    for c in range(mids):
        below = lower((fars[c] + below_top[c]).astype(BF16), down_all[c])
        for i in range(8):
            a = c * 8 + i
            adjoint[a] = (unfold(even[a] + odd[a]) + below[i]).astype(BF16)
        place = pl.ds(8 * c, 8)
        sends.append(pltpu.make_async_copy(adjoint.at[place], out.at[place], sems.at[c]))
        sends[c].start()
    wait_all(sends)


SMEM = pl.BlockSpec(memory_space=pltpu.SMEM)
VMEM = pl.BlockSpec(memory_space=pltpu.VMEM)
HBM = pl.BlockSpec(memory_space=pl.ANY)


def exchange(x):
    return lax.all_to_all(x, ("grp", "dev"), split_axis=0, concat_axis=0, tiled=True)


def swap(x):
    return lax.ppermute(x, "grp", [(g, g ^ 1) for g in range(lax.axis_size("grp"))])


def on_device(
    src_leaf,
    adj_leaf,
    up_leaf,
    up_mid,
    couple_leaf,
    couple_mid,
    couple_top,
    send_slots,
    leaf_list,
    mid_list,
    top_list,
):
    leaves, rank, nf = src_leaf.shape
    mids = up_mid.shape[0]
    peers = send_slots.shape[1]
    width = couple_leaf.shape[1]
    steps = mids
    src = jnp.swapaxes(src_leaf, 1, 2)
    adj = jnp.swapaxes(adj_leaf, 1, 2)
    slots = jnp.transpose(send_slots, (2, 0, 1))
    leaf_slots = leaf_list.T
    message = (peers, 7 * nf // 4, 2 * rank)
    chips = peers // 2
    second_message = (chips, 7 * nf // 2, 2 * rank)
    swapped_message = (chips, 3 * nf // 2, 2 * rank)
    top_shape = (chips, nf // 2, 2 * rank)
    shape = jax.ShapeDtypeStruct
    params = pltpu.CompilerParams(vmem_limit_bytes=66000000)
    roomy = pltpu.CompilerParams(vmem_limit_bytes=64000000)
    small = pl.CostEstimate(flops=10**6, bytes_accessed=10**5, transcendentals=0)

    outgoing = pl.pallas_call(
        lift_kernel,
        out_shape=shape(message, BF16),
        in_specs=[HBM] * 4,
        out_specs=HBM,
        scratch_shapes=[
            pltpu.SMEM(slots.shape, jnp.int32),
            pltpu.VMEM((leaves, nf, rank), BF16),
            pltpu.VMEM((leaves, rank, rank), BF16),
            pltpu.VMEM((mids, rank, rank), BF16),
            pltpu.VMEM(message, BF16),
            pltpu.VMEM((mids, nf, rank), BF16),
            pltpu.VMEM((2, mids, 3 * nf // 4, 2 * rank), BF16),
            pltpu.SemaphoreType.DMA((8,)),
        ],
        compiler_params=params,
        name="lift",
    )(slots, src, up_leaf, up_mid)
    arrived = exchange(outgoing)

    mid_adj, own_terms, other_terms = pl.pallas_call(
        top_kernel,
        out_shape=(shape((mids, nf, rank), BF16), shape(top_shape, F32), shape(top_shape, BF16)),
        in_specs=[SMEM] + [VMEM] * 4 + [HBM],
        out_specs=(VMEM, VMEM, VMEM),
        scratch_shapes=[pltpu.VMEM((2,) + top_shape, F32)],
        compiler_params=params,
        cost_estimate=small,
        name="top",
    )(top_list, adj, up_leaf, up_mid, couple_top, outgoing)
    swapped_terms = swap(other_terms)
    leaf_pairs_shape = (leaves, width // 2, rank, 2 * rank)
    mid_pairs_shape = (mids, width // 2, rank, 2 * rank)
    per_slot, for_other, leaf_pairs, mid_pairs = pl.pallas_call(
        adjoint_kernel,
        out_shape=(
            shape(second_message, BF16),
            shape(swapped_message, BF16),
            shape(leaf_pairs_shape, BF16),
            shape(mid_pairs_shape, BF16),
        ),
        in_specs=[HBM] * 6,
        out_specs=(HBM, HBM, HBM, HBM),
        scratch_shapes=[
            pltpu.SMEM(leaf_slots.shape, jnp.int32),
            pltpu.SMEM(mid_list.shape, jnp.int32),
            pltpu.VMEM(adj.shape, BF16),
            pltpu.VMEM(mid_adj.shape, BF16),
            pltpu.VMEM(couple_leaf.shape, BF16),
            pltpu.VMEM(couple_mid.shape, BF16),
            pltpu.VMEM(leaf_pairs_shape, BF16),
            pltpu.VMEM(mid_pairs_shape, BF16),
            pltpu.VMEM((2,) + swapped_message, BF16),
            pltpu.VMEM((3 * peers, nf // 2, 2 * rank), F32),
            pltpu.VMEM((3 * peers, nf // 2, 2 * rank), F32),
            pltpu.SemaphoreType.DMA((6,)),
            pltpu.SemaphoreType.DMA((steps,)),
            pltpu.SemaphoreType.DMA((steps,)),
            pltpu.SemaphoreType.DMA((4,)),
        ],
        compiler_params=params,
        cost_estimate=small,
        name="adjoint",
    )(leaf_slots, mid_list, adj, mid_adj, couple_leaf, couple_mid)
    top_terms = (own_terms + swapped_terms.astype(F32)).astype(BF16)
    per_slot = lax.dynamic_update_slice(per_slot, swap(for_other), (0, 3 * nf // 2, 0))
    per_slot = lax.dynamic_update_slice(per_slot, top_terms, (0, 3 * nf, 0))
    same_core = [[device_of(i, core) for i in range(chips)] for core in range(2)]
    returned = lax.all_to_all(
        per_slot, ("grp", "dev"), split_axis=0, concat_axis=0, axis_index_groups=same_core, tiled=True
    )

    own_half = arrived[:, 3 * nf // 2 :]
    other_half = swap(own_half)
    leaf_near, mid_near = pl.pallas_call(
        forward_kernel,
        out_shape=(shape((leaves, nf, rank), F32), shape((mids, nf, rank), F32)),
        in_specs=[HBM] * 5,
        out_specs=(HBM, HBM),
        scratch_shapes=[
            pltpu.SMEM(leaf_slots.shape, jnp.int32),
            pltpu.SMEM(mid_list.shape, jnp.int32),
            pltpu.VMEM(message, BF16),
            pltpu.VMEM(leaf_pairs_shape, BF16),
            pltpu.VMEM(mid_pairs_shape, BF16),
            pltpu.VMEM((leaves, nf, rank), F32),
            pltpu.VMEM((mids, nf, rank), F32),
            pltpu.VMEM((3 * peers, nf, rank), BF16),
            pltpu.SemaphoreType.DMA((4,)),
            pltpu.SemaphoreType.DMA((4,)),
            pltpu.SemaphoreType.DMA((steps,)),
            pltpu.SemaphoreType.DMA((steps,)),
        ],
        compiler_params=roomy,
        cost_estimate=small,
        name="forward",
    )(leaf_slots, mid_list, arrived, leaf_pairs, mid_pairs)
    down_shape = (mids + 1, rank, 8 * rank)
    forward, down_all = pl.pallas_call(
        finish_kernel,
        out_shape=(
            shape((leaves, nf, rank), BF16),
            shape(down_shape, BF16),
        ),
        in_specs=[SMEM] + [VMEM] * 7,
        out_specs=(VMEM, VMEM),
        compiler_params=pltpu.CompilerParams(vmem_limit_bytes=40000000),
        cost_estimate=small,
        name="finish",
    )(top_list, own_half, other_half, leaf_near, mid_near, up_leaf, up_mid, couple_top)

    adjoint = pl.pallas_call(
        lower_kernel,
        out_shape=shape((leaves, nf, rank), BF16),
        in_specs=[SMEM, VMEM, HBM],
        out_specs=HBM,
        scratch_shapes=[
            pltpu.VMEM(down_shape, BF16),
            pltpu.VMEM((leaves, nf, rank), BF16),
            pltpu.VMEM((leaves, nf // 2, 2 * rank), F32),
            pltpu.VMEM((leaves, nf // 2, 2 * rank), F32),
            pltpu.VMEM((mids, nf // 2, 2 * rank), F32),
            pltpu.VMEM((mids, nf // 2, 2 * rank), F32),
            pltpu.SemaphoreType.DMA((mids + 1,)),
        ],
        compiler_params=pltpu.CompilerParams(vmem_limit_bytes=40000000),
        name="lower",
    )(slots, returned, down_all)
    return jnp.swapaxes(forward, 1, 2), jnp.swapaxes(adjoint, 1, 2)


def solution(mesh):
    placed = (
        P(("grp", "dev"), None, None),
        P(("grp", "dev"), None, None),
        P(("grp", "dev"), None, None),
        P(("grp", "dev"), None, None),
        P(("grp", "dev"), None, None, None),
        P(("grp", "dev"), None, None, None),
        P(("grp", "dev"), None, None, None),
        P(("grp", "dev"), None, None),
        P(("grp", "dev"), None),
        P(("grp", "dev"), None),
        P(("grp", "dev"), None),
    )
    return jax.shard_map(
        on_device,
        mesh=mesh,
        in_specs=placed,
        out_specs=(P(("grp", "dev"), None, None), P(("grp", "dev"), None, None)),
        check_vma=False,
    )
```

```python
import jax
import jax.numpy as jnp
from jax import lax
from jax.experimental import pallas as pl
from jax.experimental.pallas import tpu as pltpu
from jax.sharding import PartitionSpec as P

BF16 = jnp.bfloat16
F32 = jnp.float32


def mul(x, y):
    return lax.dot_general(x, y, (((1,), (0,)), ((), ())), preferred_element_type=F32)


def mul_t(x, y):
    return lax.dot_general(x, y, (((1,), (1,)), ((), ())), preferred_element_type=F32)


def side(*blocks):
    return jnp.concatenate(blocks, axis=1)


def fold(x):
    half = x.shape[0] // 2
    return side(x[:half], x[half:])


def unfold(x):
    half = x.shape[1] // 2
    return jnp.concatenate([x[:, :half], x[:, half:]], axis=0)


def lift(rows, up, c):
    size, rank = up.shape[1:]
    return mul(side(*[rows[8 * c + i] for i in range(8)]), up[8 * c : 8 * c + 8].reshape(8 * size, rank))


def turn(up, c, eye):
    rank, size = up.shape[1:]
    return mul_t(eye, up[8 * c : 8 * c + 8].reshape(8 * rank, size)).astype(BF16)


def lower(local, down):
    rank = down.shape[0]
    below = mul(local, down)
    return [below[:, i * rank : (i + 1) * rank] for i in range(8)]


def lift_kernel(
    slots_in, src_in, up_leaf_in, up_mid_in, out, slots, src, up_leaf, up_mid, message, mid_src, tile, sems
):
    leaves, nf, rank = src.shape
    mids = up_mid.shape[0]
    parts = 4
    part = out.shape[0] // parts
    fetch_src = pltpu.make_async_copy(src_in, src, sems.at[4])
    fetch_leaf = pltpu.make_async_copy(up_leaf_in, up_leaf, sems.at[5])
    fetch_mid = pltpu.make_async_copy(up_mid_in, up_mid, sems.at[6])
    fetch_slots = pltpu.make_async_copy(slots_in, slots, sems.at[7])
    fetch_slots.start()
    fetch_src.start()
    fetch_leaf.start()
    fetch_mid.start()

    def pack_leaf(p, carry):
        message[p, :nf] = side(src[slots[0, 0, p]], src[slots[1, 0, p]])
        return carry

    fetch_slots.wait()
    fetch_src.wait()
    lax.fori_loop(0, out.shape[0], pack_leaf, 0, unroll=16)
    fetch_leaf.wait()
    for c in range(mids):
        mid_src[c] = lift(src, up_leaf, c).astype(BF16)
    fetch_mid.wait()
    top_src = lift(mid_src, up_mid, 0).astype(BF16)
    for core in range(2):
        top_half = fold(top_src[core * nf // 2 : (core + 1) * nf // 2])
        for c in range(mids):
            tile[core, c] = jnp.concatenate([fold(mid_src[c]), top_half], axis=0)

    sends = []
    for n in range(parts):
        for core in range(2):

            def pack_rest(i, carry):
                p = n * part + core * (part // 2) + i
                message[p, nf:] = tile[core, slots[2, 0, p] - leaves]
                return carry

            lax.fori_loop(0, part // 2, pack_rest, 0, unroll=16)
        place = pl.ds(n * part, part)
        sends.append(pltpu.make_async_copy(message.at[place], out.at[place], sems.at[n]))
        sends[n].start()
    wait_all(sends)


def device_of(i, core):
    return (i >> 4) * 32 + core * 16 + (i & 15)


def place_of(p):
    return (p >> 5) * 16 + (p & 15)


def top_kernel(top_list, adj, up_leaf, up_mid, couple_top, outgoing, mid_adj, own, other, total):
    rank = adj.shape[2]
    total[...] = jnp.zeros(total.shape, F32)
    for c in range(mid_adj.shape[0]):
        mid_adj[c] = lift(adj, up_leaf, c).astype(BF16)
    top_adj = lift(mid_adj, up_mid, 0).astype(BF16)
    core = lax.axis_index("grp") & 1
    for k in range(0, couple_top.shape[1], 4):
        terms = mul(top_adj, side(*[couple_top[0, k + j] for j in range(4)]))
        for j in range(4):
            p = top_list[0, k + j]
            place = ((p >> 4) & 1) ^ core
            total[place, place_of(p)] += fold(terms[:, j * rank : (j + 1) * rank])
    own[...] = total[0]
    other[...] = total[1].astype(BF16)


def start_all(copies):
    for copy in copies:
        copy.start()


def wait_all(copies):
    for copy in copies:
        copy.wait()


def adjoint_kernel(
    leaf_list_in,
    mid_list_in,
    adj_in,
    mid_adj_in,
    couple_leaf_in,
    couple_mid_in,
    out,
    other,
    leaf_pairs_out,
    mid_pairs_out,
    leaf_list,
    mid_list,
    adj,
    mid_adj,
    couple_leaf,
    couple_mid,
    leaf_pairs,
    mid_pairs,
    message,
    even,
    odd,
    sems,
    leaf_sems,
    pair_sems,
    out_sems,
):
    width, rank = couple_leaf.shape[1:3]
    nf = adj.shape[1]
    half = nf // 2
    steps = leaf_sems.shape[0]
    chunk = adj.shape[0] // steps
    is_low = lax.broadcasted_iota(jnp.int32, (half, 2 * rank), 1) < rank

    def fetch(step):
        place = pl.ds(pl.multiple_of(step * chunk, chunk), chunk)
        return pltpu.make_async_copy(couple_leaf_in.at[place], couple_leaf.at[place], leaf_sems.at[step])

    def keep_pairs(step):
        place = pl.ds(pl.multiple_of(step * chunk, chunk), chunk)
        return pltpu.make_async_copy(leaf_pairs.at[place], leaf_pairs_out.at[place], pair_sems.at[step])

    fetches = [
        pltpu.make_async_copy(leaf_list_in, leaf_list, sems.at[0]),
        pltpu.make_async_copy(mid_list_in, mid_list, sems.at[1]),
        pltpu.make_async_copy(adj_in, adj, sems.at[2]),
        pltpu.make_async_copy(mid_adj_in, mid_adj, sems.at[3]),
    ]
    fetch_mid = pltpu.make_async_copy(couple_mid_in, couple_mid, sems.at[4])
    keep_mid = pltpu.make_async_copy(mid_pairs, mid_pairs_out, sems.at[5])
    start_all(fetches)
    for step in range(steps):
        fetch(step).start()
    fetch_mid.start()

    def clear(e, carry):
        even[e] = jnp.zeros((half, 2 * rank), F32)
        odd[e] = jnp.zeros((half, 2 * rank), F32)
        return carry

    lax.fori_loop(0, even.shape[0], clear, 0, unroll=8)
    wait_all(fetches)

    def scatter(row, blocks, slot, keep):
        for k in range(0, width, 4):
            pairs = [side(blocks(k), blocks(k + 1)), side(blocks(k + 2), blocks(k + 3))]
            terms = mul(row, side(*pairs))
            for j in range(2):
                keep(k // 2 + j, pairs[j])
                pair = terms[:, 2 * j * rank : 2 * (j + 1) * rank]
                crossed = pltpu.roll(pair[half:], rank, 1)
                e, o = slot(k + 2 * j), slot(k + 2 * j + 1)
                even_sum = even[e] + jnp.where(is_low, pair[:half], crossed)
                odd_sum = odd[o] + jnp.where(is_low, crossed, pair[:half])
                even[e] = even_sum
                odd[o] = odd_sum

    def leaf_step(step, carry):
        fetch(step).wait()
        for a in range(chunk):
            g = step * chunk + a

            def keep(k, pair):
                leaf_pairs[g, k] = pair

            scatter(adj[g], lambda k: couple_leaf[g, k], lambda k: leaf_list[k, g], keep)
        keep_pairs(step).start()
        return carry

    lax.fori_loop(0, steps, leaf_step, 0)
    fetch_mid.wait()
    for c in range(mid_adj.shape[0]):

        def keep(k, pair):
            mid_pairs[c, k] = pair

        scatter(mid_adj[c], lambda k: couple_mid[c, k], lambda k: mid_list[c, k], keep)
    keep_mid.start()

    core = lax.axis_index("grp") & 1
    sends = []
    for place, target in ((1, other), (0, out)):

        def pack(i, carry):
            p = device_of(i, core ^ place)
            for s in range(3):
                e = 3 * p + s
                block = even[e] + pltpu.roll(odd[e], rank, 1)
                message[place, i, s * half : (s + 1) * half] = block.astype(BF16)
            return carry

        part = other.shape[0] // 2
        for n in range(2):
            lax.fori_loop(n * part, (n + 1) * part, pack, 0, unroll=8)
            rows = pl.ds(n * part, part)
            copy = pltpu.make_async_copy(
                message.at[place, rows], target.at[rows, pl.ds(0, 3 * half)], out_sems.at[2 * place + n]
            )
            copy.start()
            sends.append(copy)
    for step in range(steps):
        keep_pairs(step).wait()
    keep_mid.wait()
    wait_all(sends)


def gather(pairs, partner):
    near = 0
    for k in range(0, 16, 4):
        near += mul_t(side(*[partner(k + j) for j in range(4)]), side(pairs(k // 2), pairs(k // 2 + 1)))
    return near


def forward_kernel(
    leaf_list_in,
    mid_list_in,
    arrived_in,
    leaf_pairs_in,
    mid_pairs_in,
    leaf_near_out,
    mid_near_out,
    leaf_list,
    mid_list,
    arrived,
    leaf_pairs,
    mid_pairs,
    leaf_near,
    mid_near,
    coeff,
    sems,
    arrived_sems,
    leaf_sems,
    near_sems,
):
    leaves, nf, rank = leaf_near.shape
    steps = leaf_sems.shape[0]
    chunk = leaves // steps
    parts = arrived_sems.shape[0]
    part = arrived.shape[0] // parts

    def place(step):
        return pl.ds(pl.multiple_of(step * chunk, chunk), chunk)

    def fetch(step):
        return pltpu.make_async_copy(leaf_pairs_in.at[place(step)], leaf_pairs.at[place(step)], leaf_sems.at[step])

    def keep(step):
        return pltpu.make_async_copy(leaf_near.at[place(step)], leaf_near_out.at[place(step)], near_sems.at[step])

    lists = [
        pltpu.make_async_copy(leaf_list_in, leaf_list, sems.at[0]),
        pltpu.make_async_copy(mid_list_in, mid_list, sems.at[1]),
    ]
    messages = []
    for n in range(parts):
        rows_n = pl.ds(n * part, part)
        messages.append(pltpu.make_async_copy(arrived_in.at[rows_n], arrived.at[rows_n], arrived_sems.at[n]))
    fetch_mid = pltpu.make_async_copy(mid_pairs_in, mid_pairs, sems.at[2])
    keep_mid = pltpu.make_async_copy(mid_near, mid_near_out, sems.at[3])
    start_all(messages)
    start_all(lists)
    for step in range(steps):
        fetch(step).start()
    fetch_mid.start()

    def unpack(p, carry):
        pair = arrived[p, :nf]
        coeff[3 * p] = pair[:, :rank]
        coeff[3 * p + 1] = pair[:, rank:]
        coeff[3 * p + 2] = unfold(arrived[p, nf : nf + nf // 2])
        return carry

    for n in range(parts):
        messages[n].wait()
        lax.fori_loop(n * part, (n + 1) * part, unpack, 0, unroll=8)
    wait_all(lists)

    def leaf_step(step, carry):
        fetch(step).wait()
        for a in range(chunk):
            g = step * chunk + a
            leaf_near[g] = gather(lambda k: leaf_pairs[g, k], lambda k: coeff[leaf_list[k, g]])
        keep(step).start()
        return carry

    lax.fori_loop(0, steps, leaf_step, 0)
    fetch_mid.wait()
    for c in range(mid_near.shape[0]):
        mid_near[c] = gather(lambda k: mid_pairs[c, k], lambda k: coeff[mid_list[c, k]])
    keep_mid.start()
    for step in range(steps):
        keep(step).wait()
    keep_mid.wait()


def finish_kernel(
    top_list, own_half, other_half, leaf_near, mid_near, up_leaf, up_mid, couple_top, forward, down_out, down_all, sem
):
    nf, rank = forward.shape[1:]
    shape = (rank, rank)
    eye = (lax.broadcasted_iota(jnp.int32, shape, 0) == lax.broadcasted_iota(jnp.int32, shape, 1)).astype(BF16)

    def partner(k):
        j = top_list[0, k]
        return jnp.concatenate([unfold(own_half[j]), unfold(other_half[j])], axis=0)

    near = gather(lambda k: side(couple_top[0, 2 * k], couple_top[0, 2 * k + 1]), partner)
    swapped = jnp.concatenate([near[nf // 2 :], near[: nf // 2]], axis=0)
    core = lax.axis_index("grp") % 2
    mids = mid_near.shape[0]
    down_all[mids] = turn(up_mid, 0, eye)
    below_top = lower(jnp.where(core == 0, near, swapped).astype(BF16), down_all[mids])
    for c in range(mids):
        down = turn(up_leaf, c, eye)
        down_all[c] = down
        below = lower((mid_near[c] + below_top[c]).astype(BF16), down)
        for i in range(8):
            forward[8 * c + i] = (leaf_near[8 * c + i] + below[i]).astype(BF16)
    keep = pltpu.make_async_copy(down_all, down_out.at[pl.ds(0, mids + 1)], sem)
    keep.start()
    keep.wait()


def lower_kernel(
    slots, returned, down_all_in, out, down_all, adjoint, even, odd, even_mid, odd_mid, sems
):
    leaves, nf, rank = adjoint.shape
    mids = even_mid.shape[0]
    fetch = pltpu.make_async_copy(down_all_in.at[pl.ds(0, mids + 1)], down_all, sems.at[mids])
    fetch.start()
    for far in (even, odd, even_mid, odd_mid):
        far[...] = jnp.zeros(far.shape, F32)
    half = nf // 2
    core = lax.axis_index("grp") & 1

    def collect(i, top):
        sums = []
        for place, far, far_mid in ((0, even, even_mid), (1, odd, odd_mid)):
            p = device_of(i, core ^ place)
            for s, held in ((0, far), (1, far), (2, far_mid)):
                u = slots[s, 0, p] - (leaves if s == 2 else 0)
                first = (3 * place + s) * half
                sums.append((held, u, held[u] + returned[i, first : first + half].astype(F32)))
        for held, u, value in sums:
            held[u] = value
        return top + returned[i, 6 * half :].astype(F32)

    top = lax.fori_loop(0, returned.shape[0], collect, jnp.zeros((half, 2 * rank), F32), unroll=8)
    fars = [unfold(even_mid[c] + odd_mid[c]) for c in range(mids)]
    fetch.wait()
    below_top = lower(unfold(top).astype(BF16), down_all[mids])
    sends = []
    for c in range(mids):
        below = lower((fars[c] + below_top[c]).astype(BF16), down_all[c])
        for i in range(8):
            a = c * 8 + i
            adjoint[a] = (unfold(even[a] + odd[a]) + below[i]).astype(BF16)
        place = pl.ds(8 * c, 8)
        sends.append(pltpu.make_async_copy(adjoint.at[place], out.at[place], sems.at[c]))
        sends[c].start()
    wait_all(sends)


SMEM = pl.BlockSpec(memory_space=pltpu.SMEM)
VMEM = pl.BlockSpec(memory_space=pltpu.VMEM)
HBM = pl.BlockSpec(memory_space=pl.ANY)


def exchange(x):
    return lax.all_to_all(x, ("grp", "dev"), split_axis=0, concat_axis=0, tiled=True)


def swap(x):
    return lax.ppermute(x, "grp", [(g, g ^ 1) for g in range(lax.axis_size("grp"))])


def on_device(
    src_leaf,
    adj_leaf,
    up_leaf,
    up_mid,
    couple_leaf,
    couple_mid,
    couple_top,
    send_slots,
    leaf_list,
    mid_list,
    top_list,
):
    leaves, rank, nf = src_leaf.shape
    mids = up_mid.shape[0]
    peers = send_slots.shape[1]
    width = couple_leaf.shape[1]
    steps = mids
    src = jnp.swapaxes(src_leaf, 1, 2)
    adj = jnp.swapaxes(adj_leaf, 1, 2)
    slots = jnp.transpose(send_slots, (2, 0, 1))
    leaf_slots = leaf_list.T
    message = (peers, 7 * nf // 4, 2 * rank)
    chips = peers // 2
    second_message = (chips, 7 * nf // 2, 2 * rank)
    swapped_message = (chips, 3 * nf // 2, 2 * rank)
    top_shape = (chips, nf // 2, 2 * rank)
    shape = jax.ShapeDtypeStruct
    params = pltpu.CompilerParams(vmem_limit_bytes=66000000)
    roomy = pltpu.CompilerParams(vmem_limit_bytes=64000000)
    small = pl.CostEstimate(flops=10**6, bytes_accessed=10**5, transcendentals=0)

    outgoing = pl.pallas_call(
        lift_kernel,
        out_shape=shape(message, BF16),
        in_specs=[HBM] * 4,
        out_specs=HBM,
        scratch_shapes=[
            pltpu.SMEM(slots.shape, jnp.int32),
            pltpu.VMEM((leaves, nf, rank), BF16),
            pltpu.VMEM((leaves, rank, rank), BF16),
            pltpu.VMEM((mids, rank, rank), BF16),
            pltpu.VMEM(message, BF16),
            pltpu.VMEM((mids, nf, rank), BF16),
            pltpu.VMEM((2, mids, 3 * nf // 4, 2 * rank), BF16),
            pltpu.SemaphoreType.DMA((8,)),
        ],
        compiler_params=params,
        name="lift",
    )(slots, src, up_leaf, up_mid)
    arrived = exchange(outgoing)

    mid_adj, own_terms, other_terms = pl.pallas_call(
        top_kernel,
        out_shape=(shape((mids, nf, rank), BF16), shape(top_shape, F32), shape(top_shape, BF16)),
        in_specs=[SMEM] + [VMEM] * 4 + [HBM],
        out_specs=(VMEM, VMEM, VMEM),
        scratch_shapes=[pltpu.VMEM((2,) + top_shape, F32)],
        compiler_params=params,
        cost_estimate=small,
        name="top",
    )(top_list, adj, up_leaf, up_mid, couple_top, outgoing)
    swapped_terms = swap(other_terms)
    leaf_pairs_shape = (leaves, width // 2, rank, 2 * rank)
    mid_pairs_shape = (mids, width // 2, rank, 2 * rank)
    per_slot, for_other, leaf_pairs, mid_pairs = pl.pallas_call(
        adjoint_kernel,
        out_shape=(
            shape(second_message, BF16),
            shape(swapped_message, BF16),
            shape(leaf_pairs_shape, BF16),
            shape(mid_pairs_shape, BF16),
        ),
        in_specs=[HBM] * 6,
        out_specs=(HBM, HBM, HBM, HBM),
        scratch_shapes=[
            pltpu.SMEM(leaf_slots.shape, jnp.int32),
            pltpu.SMEM(mid_list.shape, jnp.int32),
            pltpu.VMEM(adj.shape, BF16),
            pltpu.VMEM(mid_adj.shape, BF16),
            pltpu.VMEM(couple_leaf.shape, BF16),
            pltpu.VMEM(couple_mid.shape, BF16),
            pltpu.VMEM(leaf_pairs_shape, BF16),
            pltpu.VMEM(mid_pairs_shape, BF16),
            pltpu.VMEM((2,) + swapped_message, BF16),
            pltpu.VMEM((3 * peers, nf // 2, 2 * rank), F32),
            pltpu.VMEM((3 * peers, nf // 2, 2 * rank), F32),
            pltpu.SemaphoreType.DMA((6,)),
            pltpu.SemaphoreType.DMA((steps,)),
            pltpu.SemaphoreType.DMA((steps,)),
            pltpu.SemaphoreType.DMA((4,)),
        ],
        compiler_params=params,
        cost_estimate=small,
        name="adjoint",
    )(leaf_slots, mid_list, adj, mid_adj, couple_leaf, couple_mid)
    top_terms = (own_terms + swapped_terms.astype(F32)).astype(BF16)
    per_slot = lax.dynamic_update_slice(per_slot, swap(for_other), (0, 3 * nf // 2, 0))
    per_slot = lax.dynamic_update_slice(per_slot, top_terms, (0, 3 * nf, 0))
    same_core = [[device_of(i, core) for i in range(chips)] for core in range(2)]
    returned = lax.all_to_all(
        per_slot, ("grp", "dev"), split_axis=0, concat_axis=0, axis_index_groups=same_core, tiled=True
    )

    own_half = arrived[:, 3 * nf // 2 :]
    other_half = swap(own_half)
    leaf_near, mid_near = pl.pallas_call(
        forward_kernel,
        out_shape=(shape((leaves, nf, rank), F32), shape((mids, nf, rank), F32)),
        in_specs=[HBM] * 5,
        out_specs=(HBM, HBM),
        scratch_shapes=[
            pltpu.SMEM(leaf_slots.shape, jnp.int32),
            pltpu.SMEM(mid_list.shape, jnp.int32),
            pltpu.VMEM(message, BF16),
            pltpu.VMEM(leaf_pairs_shape, BF16),
            pltpu.VMEM(mid_pairs_shape, BF16),
            pltpu.VMEM((leaves, nf, rank), F32),
            pltpu.VMEM((mids, nf, rank), F32),
            pltpu.VMEM((3 * peers, nf, rank), BF16),
            pltpu.SemaphoreType.DMA((4,)),
            pltpu.SemaphoreType.DMA((4,)),
            pltpu.SemaphoreType.DMA((steps,)),
            pltpu.SemaphoreType.DMA((steps,)),
        ],
        compiler_params=roomy,
        cost_estimate=small,
        name="forward",
    )(leaf_slots, mid_list, arrived, leaf_pairs, mid_pairs)
    down_shape = (mids + 1, rank, 8 * rank)
    forward, down_all = pl.pallas_call(
        finish_kernel,
        out_shape=(
            shape((leaves, nf, rank), BF16),
            shape((50 * mids,) + down_shape[1:], BF16),
        ),
        in_specs=[SMEM] + [VMEM] * 7,
        out_specs=(VMEM, HBM),
        scratch_shapes=[pltpu.VMEM(down_shape, BF16), pltpu.SemaphoreType.DMA],
        compiler_params=roomy,
        cost_estimate=small,
        name="finish",
    )(top_list, own_half, other_half, leaf_near, mid_near, up_leaf, up_mid, couple_top)

    adjoint = pl.pallas_call(
        lower_kernel,
        out_shape=shape((leaves, nf, rank), BF16),
        in_specs=[SMEM, VMEM, HBM],
        out_specs=HBM,
        scratch_shapes=[
            pltpu.VMEM(down_shape, BF16),
            pltpu.VMEM((leaves, nf, rank), BF16),
            pltpu.VMEM((leaves, nf // 2, 2 * rank), F32),
            pltpu.VMEM((leaves, nf // 2, 2 * rank), F32),
            pltpu.VMEM((mids, nf // 2, 2 * rank), F32),
            pltpu.VMEM((mids, nf // 2, 2 * rank), F32),
            pltpu.SemaphoreType.DMA((mids + 1,)),
        ],
        compiler_params=pltpu.CompilerParams(vmem_limit_bytes=42000000),
        name="lower",
    )(slots, returned, down_all)
    return jnp.swapaxes(forward, 1, 2), jnp.swapaxes(adjoint, 1, 2)


def solution(mesh):
    placed = (
        P(("grp", "dev"), None, None),
        P(("grp", "dev"), None, None),
        P(("grp", "dev"), None, None),
        P(("grp", "dev"), None, None),
        P(("grp", "dev"), None, None, None),
        P(("grp", "dev"), None, None, None),
        P(("grp", "dev"), None, None, None),
        P(("grp", "dev"), None, None),
        P(("grp", "dev"), None),
        P(("grp", "dev"), None),
        P(("grp", "dev"), None),
    )
    return jax.shard_map(
        on_device,
        mesh=mesh,
        in_specs=placed,
        out_specs=(P(("grp", "dev"), None, None), P(("grp", "dev"), None, None)),
        check_vma=False,
    )
```

```python
import jax
import jax.numpy as jnp
from jax import lax
from jax.experimental import pallas as pl
from jax.experimental.pallas import tpu as pltpu
from jax.sharding import PartitionSpec as P

BF16 = jnp.bfloat16
F32 = jnp.float32


def mul(x, y):
    return lax.dot_general(x, y, (((1,), (0,)), ((), ())), preferred_element_type=F32)


def mul_t(x, y):
    return lax.dot_general(x, y, (((1,), (1,)), ((), ())), preferred_element_type=F32)


def side(*blocks):
    return jnp.concatenate(blocks, axis=1)


def fold(x):
    half = x.shape[0] // 2
    return side(x[:half], x[half:])


def unfold(x):
    half = x.shape[1] // 2
    return jnp.concatenate([x[:, :half], x[:, half:]], axis=0)


def lift(rows, up, c):
    size, rank = up.shape[1:]
    return mul(side(*[rows[8 * c + i] for i in range(8)]), up[8 * c : 8 * c + 8].reshape(8 * size, rank))


def turn(up, c, eye):
    rank, size = up.shape[1:]
    return mul_t(eye, up[8 * c : 8 * c + 8].reshape(8 * rank, size)).astype(BF16)


def lower(local, down):
    rank = down.shape[0]
    below = mul(local, down)
    return [below[:, i * rank : (i + 1) * rank] for i in range(8)]


def lift_kernel(
    slots_in, src_in, up_leaf_in, up_mid_in, out, slots, src, up_leaf, up_mid, message, mid_src, tile, sems
):
    leaves, nf, rank = src.shape
    mids = up_mid.shape[0]
    parts = 8
    part = out.shape[0] // parts
    fetch_src = pltpu.make_async_copy(src_in, src, sems.at[8])
    fetch_leaf = pltpu.make_async_copy(up_leaf_in, up_leaf, sems.at[9])
    fetch_mid = pltpu.make_async_copy(up_mid_in, up_mid, sems.at[10])
    fetch_slots = pltpu.make_async_copy(slots_in, slots, sems.at[11])
    fetch_slots.start()
    fetch_src.start()
    fetch_leaf.start()
    fetch_mid.start()

    def pack_leaf(p, carry):
        message[p, :nf] = side(src[slots[0, 0, p]], src[slots[1, 0, p]])
        return carry

    fetch_slots.wait()
    fetch_src.wait()
    lax.fori_loop(0, out.shape[0], pack_leaf, 0, unroll=16)
    fetch_leaf.wait()
    for c in range(mids):
        mid_src[c] = lift(src, up_leaf, c).astype(BF16)
    fetch_mid.wait()
    top_src = lift(mid_src, up_mid, 0).astype(BF16)
    for core in range(2):
        top_half = fold(top_src[core * nf // 2 : (core + 1) * nf // 2])
        for c in range(mids):
            tile[core, c] = jnp.concatenate([fold(mid_src[c]), top_half], axis=0)

    sends = []
    for n in range(parts):
        core = n & 1

        def pack_rest(p, carry):
            message[p, nf:] = tile[core, slots[2, 0, p] - leaves]
            return carry

        lax.fori_loop(n * part, (n + 1) * part, pack_rest, 0, unroll=16)
        place = pl.ds(n * part, part)
        sends.append(pltpu.make_async_copy(message.at[place], out.at[place], sems.at[n]))
        sends[n].start()
    wait_all(sends)


def device_of(i, core):
    return (i >> 4) * 32 + core * 16 + (i & 15)


def place_of(p):
    return (p >> 5) * 16 + (p & 15)


def top_kernel(top_list, adj, up_leaf, up_mid, couple_top, outgoing, mid_adj, own, other, total):
    rank = adj.shape[2]
    total[...] = jnp.zeros(total.shape, F32)
    for c in range(mid_adj.shape[0]):
        mid_adj[c] = lift(adj, up_leaf, c).astype(BF16)
    top_adj = lift(mid_adj, up_mid, 0).astype(BF16)
    core = lax.axis_index("grp") & 1
    for k in range(0, couple_top.shape[1], 4):
        terms = mul(top_adj, side(*[couple_top[0, k + j] for j in range(4)]))
        for j in range(4):
            p = top_list[0, k + j]
            place = ((p >> 4) & 1) ^ core
            total[place, place_of(p)] += fold(terms[:, j * rank : (j + 1) * rank])
    own[...] = total[0]
    other[...] = total[1].astype(BF16)


def start_all(copies):
    for copy in copies:
        copy.start()


def wait_all(copies):
    for copy in copies:
        copy.wait()


def adjoint_kernel(
    leaf_list_in,
    mid_list_in,
    adj_in,
    mid_adj_in,
    couple_leaf_in,
    couple_mid_in,
    out,
    other,
    leaf_pairs_out,
    mid_pairs_out,
    leaf_list,
    mid_list,
    adj,
    mid_adj,
    couple_leaf,
    couple_mid,
    leaf_pairs,
    mid_pairs,
    message,
    even,
    odd,
    sems,
    leaf_sems,
    pair_sems,
    out_sems,
):
    width, rank = couple_leaf.shape[1:3]
    nf = adj.shape[1]
    half = nf // 2
    steps = leaf_sems.shape[0]
    chunk = adj.shape[0] // steps
    is_low = lax.broadcasted_iota(jnp.int32, (half, 2 * rank), 1) < rank

    def fetch(step):
        place = pl.ds(pl.multiple_of(step * chunk, chunk), chunk)
        return pltpu.make_async_copy(couple_leaf_in.at[place], couple_leaf.at[place], leaf_sems.at[step])

    def keep_pairs(step):
        place = pl.ds(pl.multiple_of(step * chunk, chunk), chunk)
        return pltpu.make_async_copy(leaf_pairs.at[place], leaf_pairs_out.at[place], pair_sems.at[step])

    fetches = [
        pltpu.make_async_copy(leaf_list_in, leaf_list, sems.at[0]),
        pltpu.make_async_copy(mid_list_in, mid_list, sems.at[1]),
        pltpu.make_async_copy(adj_in, adj, sems.at[2]),
        pltpu.make_async_copy(mid_adj_in, mid_adj, sems.at[3]),
    ]
    fetch_mid = pltpu.make_async_copy(couple_mid_in, couple_mid, sems.at[4])
    keep_mid = pltpu.make_async_copy(mid_pairs, mid_pairs_out, sems.at[5])
    start_all(fetches)
    for step in range(steps):
        fetch(step).start()
    fetch_mid.start()

    def clear(e, carry):
        even[e] = jnp.zeros((half, 2 * rank), F32)
        odd[e] = jnp.zeros((half, 2 * rank), F32)
        return carry

    lax.fori_loop(0, even.shape[0], clear, 0, unroll=8)
    wait_all(fetches)

    def scatter(row, blocks, slot, keep):
        for k in range(0, width, 4):
            pairs = [side(blocks(k), blocks(k + 1)), side(blocks(k + 2), blocks(k + 3))]
            terms = mul(row, side(*pairs))
            for j in range(2):
                keep(k // 2 + j, pairs[j])
                pair = terms[:, 2 * j * rank : 2 * (j + 1) * rank]
                crossed = pltpu.roll(pair[half:], rank, 1)
                e, o = slot(k + 2 * j), slot(k + 2 * j + 1)
                even_sum = even[e] + jnp.where(is_low, pair[:half], crossed)
                odd_sum = odd[o] + jnp.where(is_low, crossed, pair[:half])
                even[e] = even_sum
                odd[o] = odd_sum

    def leaf_step(step, carry):
        fetch(step).wait()
        for a in range(chunk):
            g = step * chunk + a

            def keep(k, pair):
                leaf_pairs[g, k] = pair

            scatter(adj[g], lambda k: couple_leaf[g, k], lambda k: leaf_list[k, g], keep)
        keep_pairs(step).start()
        return carry

    lax.fori_loop(0, steps, leaf_step, 0)
    fetch_mid.wait()
    for c in range(mid_adj.shape[0]):

        def keep(k, pair):
            mid_pairs[c, k] = pair

        scatter(mid_adj[c], lambda k: couple_mid[c, k], lambda k: mid_list[c, k], keep)
    keep_mid.start()

    core = lax.axis_index("grp") & 1
    sends = []
    for place, target in ((1, other), (0, out)):

        def pack(i, carry):
            p = device_of(i, core ^ place)
            for s in range(3):
                e = 3 * p + s
                block = even[e] + pltpu.roll(odd[e], rank, 1)
                message[place, i, s * half : (s + 1) * half] = block.astype(BF16)
            return carry

        part = other.shape[0] // 2
        for n in range(2):
            lax.fori_loop(n * part, (n + 1) * part, pack, 0, unroll=8)
            rows = pl.ds(n * part, part)
            copy = pltpu.make_async_copy(
                message.at[place, rows], target.at[rows, pl.ds(0, 3 * half)], out_sems.at[2 * place + n]
            )
            copy.start()
            sends.append(copy)
    for step in range(steps):
        keep_pairs(step).wait()
    keep_mid.wait()
    wait_all(sends)


def gather(pairs, partner):
    near = 0
    for k in range(0, 16, 4):
        near += mul_t(side(*[partner(k + j) for j in range(4)]), side(pairs(k // 2), pairs(k // 2 + 1)))
    return near


def forward_kernel(
    leaf_list_in,
    mid_list_in,
    arrived_in,
    leaf_pairs_in,
    mid_pairs_in,
    leaf_near_out,
    mid_near_out,
    leaf_list,
    mid_list,
    arrived,
    leaf_pairs,
    mid_pairs,
    leaf_near,
    mid_near,
    coeff,
    sems,
    arrived_sems,
    leaf_sems,
    near_sems,
):
    leaves, nf, rank = leaf_near.shape
    steps = leaf_sems.shape[0]
    chunk = leaves // steps
    parts = arrived_sems.shape[0]
    part = arrived.shape[0] // parts

    def place(step):
        return pl.ds(pl.multiple_of(step * chunk, chunk), chunk)

    def fetch(step):
        return pltpu.make_async_copy(leaf_pairs_in.at[place(step)], leaf_pairs.at[place(step)], leaf_sems.at[step])

    def keep(step):
        return pltpu.make_async_copy(leaf_near.at[place(step)], leaf_near_out.at[place(step)], near_sems.at[step])

    lists = [
        pltpu.make_async_copy(leaf_list_in, leaf_list, sems.at[0]),
        pltpu.make_async_copy(mid_list_in, mid_list, sems.at[1]),
    ]
    messages = []
    for n in range(parts):
        rows_n = pl.ds(n * part, part)
        messages.append(pltpu.make_async_copy(arrived_in.at[rows_n], arrived.at[rows_n], arrived_sems.at[n]))
    fetch_mid = pltpu.make_async_copy(mid_pairs_in, mid_pairs, sems.at[2])
    keep_mid = pltpu.make_async_copy(mid_near, mid_near_out, sems.at[3])
    start_all(messages)
    start_all(lists)
    for step in range(steps):
        fetch(step).start()
    fetch_mid.start()

    def unpack(p, carry):
        pair = arrived[p, :nf]
        coeff[3 * p] = pair[:, :rank]
        coeff[3 * p + 1] = pair[:, rank:]
        coeff[3 * p + 2] = unfold(arrived[p, nf : nf + nf // 2])
        return carry

    for n in range(parts):
        messages[n].wait()
        lax.fori_loop(n * part, (n + 1) * part, unpack, 0, unroll=8)
    wait_all(lists)

    def leaf_step(step, carry):
        fetch(step).wait()
        for a in range(chunk):
            g = step * chunk + a
            leaf_near[g] = gather(lambda k: leaf_pairs[g, k], lambda k: coeff[leaf_list[k, g]])
        keep(step).start()
        return carry

    lax.fori_loop(0, steps, leaf_step, 0)
    fetch_mid.wait()
    for c in range(mid_near.shape[0]):
        mid_near[c] = gather(lambda k: mid_pairs[c, k], lambda k: coeff[mid_list[c, k]])
    keep_mid.start()
    for step in range(steps):
        keep(step).wait()
    keep_mid.wait()


def finish_kernel(
    top_list, own_half, other_half, leaf_near, mid_near, up_leaf, up_mid, couple_top, forward, down_out, down_all, sem
):
    nf, rank = forward.shape[1:]
    shape = (rank, rank)
    eye = (lax.broadcasted_iota(jnp.int32, shape, 0) == lax.broadcasted_iota(jnp.int32, shape, 1)).astype(BF16)

    def partner(k):
        j = top_list[0, k]
        return jnp.concatenate([unfold(own_half[j]), unfold(other_half[j])], axis=0)

    near = gather(lambda k: side(couple_top[0, 2 * k], couple_top[0, 2 * k + 1]), partner)
    swapped = jnp.concatenate([near[nf // 2 :], near[: nf // 2]], axis=0)
    core = lax.axis_index("grp") % 2
    mids = mid_near.shape[0]
    down_all[mids] = turn(up_mid, 0, eye)
    below_top = lower(jnp.where(core == 0, near, swapped).astype(BF16), down_all[mids])
    for c in range(mids):
        down = turn(up_leaf, c, eye)
        down_all[c] = down
        below = lower((mid_near[c] + below_top[c]).astype(BF16), down)
        for i in range(8):
            forward[8 * c + i] = (leaf_near[8 * c + i] + below[i]).astype(BF16)
    keep = pltpu.make_async_copy(down_all, down_out.at[pl.ds(0, mids + 1)], sem)
    keep.start()
    keep.wait()


def lower_kernel(
    slots, returned, down_all_in, out, down_all, adjoint, even, odd, even_mid, odd_mid, sems
):
    leaves, nf, rank = adjoint.shape
    mids = even_mid.shape[0]
    fetch = pltpu.make_async_copy(down_all_in.at[pl.ds(0, mids + 1)], down_all, sems.at[mids])
    fetch.start()
    for far in (even, odd, even_mid, odd_mid):
        far[...] = jnp.zeros(far.shape, F32)
    half = nf // 2
    core = lax.axis_index("grp") & 1

    def collect(i, top):
        sums = []
        for place, far, far_mid in ((0, even, even_mid), (1, odd, odd_mid)):
            p = device_of(i, core ^ place)
            for s, held in ((0, far), (1, far), (2, far_mid)):
                u = slots[s, 0, p] - (leaves if s == 2 else 0)
                first = (3 * place + s) * half
                sums.append((held, u, held[u] + returned[i, first : first + half].astype(F32)))
        for held, u, value in sums:
            held[u] = value
        return top + returned[i, 6 * half :].astype(F32)

    top = lax.fori_loop(0, returned.shape[0], collect, jnp.zeros((half, 2 * rank), F32), unroll=16)
    fars = [unfold(even_mid[c] + odd_mid[c]) for c in range(mids)]
    fetch.wait()
    below_top = lower(unfold(top).astype(BF16), down_all[mids])
    sends = []
    for c in range(mids):
        below = lower((fars[c] + below_top[c]).astype(BF16), down_all[c])
        for i in range(8):
            a = c * 8 + i
            adjoint[a] = (unfold(even[a] + odd[a]) + below[i]).astype(BF16)
        place = pl.ds(8 * c, 8)
        sends.append(pltpu.make_async_copy(adjoint.at[place], out.at[place], sems.at[c]))
        sends[c].start()
    wait_all(sends)


SMEM = pl.BlockSpec(memory_space=pltpu.SMEM)
VMEM = pl.BlockSpec(memory_space=pltpu.VMEM)
HBM = pl.BlockSpec(memory_space=pl.ANY)


def exchange(x):
    return lax.all_to_all(x, ("grp", "dev"), split_axis=0, concat_axis=0, tiled=True)


def swap(x):
    return lax.ppermute(x, "grp", [(g, g ^ 1) for g in range(lax.axis_size("grp"))])


def on_device(
    src_leaf,
    adj_leaf,
    up_leaf,
    up_mid,
    couple_leaf,
    couple_mid,
    couple_top,
    send_slots,
    leaf_list,
    mid_list,
    top_list,
):
    leaves, rank, nf = src_leaf.shape
    mids = up_mid.shape[0]
    peers = send_slots.shape[1]
    width = couple_leaf.shape[1]
    steps = mids
    src = jnp.swapaxes(src_leaf, 1, 2)
    adj = jnp.swapaxes(adj_leaf, 1, 2)
    slots = jnp.transpose(send_slots, (2, 0, 1))
    leaf_slots = leaf_list.T
    message = (peers, 7 * nf // 4, 2 * rank)
    chips = peers // 2
    second_message = (chips, 7 * nf // 2, 2 * rank)
    swapped_message = (chips, 3 * nf // 2, 2 * rank)
    top_shape = (chips, nf // 2, 2 * rank)
    shape = jax.ShapeDtypeStruct
    params = pltpu.CompilerParams(vmem_limit_bytes=66000000)
    roomy = pltpu.CompilerParams(vmem_limit_bytes=64000000)
    small = pl.CostEstimate(flops=10**6, bytes_accessed=10**5, transcendentals=0)

    outgoing = pl.pallas_call(
        lift_kernel,
        out_shape=shape(message, BF16),
        in_specs=[HBM] * 4,
        out_specs=HBM,
        scratch_shapes=[
            pltpu.SMEM(slots.shape, jnp.int32),
            pltpu.VMEM((leaves, nf, rank), BF16),
            pltpu.VMEM((leaves, rank, rank), BF16),
            pltpu.VMEM((mids, rank, rank), BF16),
            pltpu.VMEM(message, BF16),
            pltpu.VMEM((mids, nf, rank), BF16),
            pltpu.VMEM((2, mids, 3 * nf // 4, 2 * rank), BF16),
            pltpu.SemaphoreType.DMA((12,)),
        ],
        compiler_params=params,
        name="lift",
    )(slots, src, up_leaf, up_mid)
    arrived = exchange(outgoing)

    mid_adj, own_terms, other_terms = pl.pallas_call(
        top_kernel,
        out_shape=(shape((mids, nf, rank), BF16), shape(top_shape, F32), shape(top_shape, BF16)),
        in_specs=[SMEM] + [VMEM] * 4 + [HBM],
        out_specs=(VMEM, VMEM, VMEM),
        scratch_shapes=[pltpu.VMEM((2,) + top_shape, F32)],
        compiler_params=params,
        cost_estimate=small,
        name="top",
    )(top_list, adj, up_leaf, up_mid, couple_top, outgoing)
    swapped_terms = swap(other_terms)
    leaf_pairs_shape = (leaves, width // 2, rank, 2 * rank)
    mid_pairs_shape = (mids, width // 2, rank, 2 * rank)
    per_slot, for_other, leaf_pairs, mid_pairs = pl.pallas_call(
        adjoint_kernel,
        out_shape=(
            shape(second_message, BF16),
            shape(swapped_message, BF16),
            shape(leaf_pairs_shape, BF16),
            shape(mid_pairs_shape, BF16),
        ),
        in_specs=[HBM] * 6,
        out_specs=(HBM, HBM, HBM, HBM),
        scratch_shapes=[
            pltpu.SMEM(leaf_slots.shape, jnp.int32),
            pltpu.SMEM(mid_list.shape, jnp.int32),
            pltpu.VMEM(adj.shape, BF16),
            pltpu.VMEM(mid_adj.shape, BF16),
            pltpu.VMEM(couple_leaf.shape, BF16),
            pltpu.VMEM(couple_mid.shape, BF16),
            pltpu.VMEM(leaf_pairs_shape, BF16),
            pltpu.VMEM(mid_pairs_shape, BF16),
            pltpu.VMEM((2,) + swapped_message, BF16),
            pltpu.VMEM((3 * peers, nf // 2, 2 * rank), F32),
            pltpu.VMEM((3 * peers, nf // 2, 2 * rank), F32),
            pltpu.SemaphoreType.DMA((6,)),
            pltpu.SemaphoreType.DMA((steps,)),
            pltpu.SemaphoreType.DMA((steps,)),
            pltpu.SemaphoreType.DMA((4,)),
        ],
        compiler_params=params,
        cost_estimate=small,
        name="adjoint",
    )(leaf_slots, mid_list, adj, mid_adj, couple_leaf, couple_mid)
    top_terms = (own_terms + swapped_terms.astype(F32)).astype(BF16)
    per_slot = lax.dynamic_update_slice(per_slot, swap(for_other), (0, 3 * nf // 2, 0))
    per_slot = lax.dynamic_update_slice(per_slot, top_terms, (0, 3 * nf, 0))
    same_core = [[device_of(i, core) for i in range(chips)] for core in range(2)]
    returned = lax.all_to_all(
        per_slot, ("grp", "dev"), split_axis=0, concat_axis=0, axis_index_groups=same_core, tiled=True
    )

    own_half = arrived[:, 3 * nf // 2 :]
    other_half = swap(own_half)
    leaf_near, mid_near = pl.pallas_call(
        forward_kernel,
        out_shape=(shape((leaves, nf, rank), F32), shape((mids, nf, rank), F32)),
        in_specs=[HBM] * 5,
        out_specs=(HBM, HBM),
        scratch_shapes=[
            pltpu.SMEM(leaf_slots.shape, jnp.int32),
            pltpu.SMEM(mid_list.shape, jnp.int32),
            pltpu.VMEM(message, BF16),
            pltpu.VMEM(leaf_pairs_shape, BF16),
            pltpu.VMEM(mid_pairs_shape, BF16),
            pltpu.VMEM((leaves, nf, rank), F32),
            pltpu.VMEM((mids, nf, rank), F32),
            pltpu.VMEM((3 * peers, nf, rank), BF16),
            pltpu.SemaphoreType.DMA((4,)),
            pltpu.SemaphoreType.DMA((4,)),
            pltpu.SemaphoreType.DMA((steps,)),
            pltpu.SemaphoreType.DMA((steps,)),
        ],
        compiler_params=roomy,
        cost_estimate=small,
        name="forward",
    )(leaf_slots, mid_list, arrived, leaf_pairs, mid_pairs)
    down_shape = (mids + 1, rank, 8 * rank)
    forward, down_all = pl.pallas_call(
        finish_kernel,
        out_shape=(
            shape((leaves, nf, rank), BF16),
            shape((50 * mids,) + down_shape[1:], BF16),
        ),
        in_specs=[SMEM] + [VMEM] * 7,
        out_specs=(VMEM, HBM),
        scratch_shapes=[pltpu.VMEM(down_shape, BF16), pltpu.SemaphoreType.DMA],
        compiler_params=roomy,
        cost_estimate=small,
        name="finish",
    )(top_list, own_half, other_half, leaf_near, mid_near, up_leaf, up_mid, couple_top)

    adjoint = pl.pallas_call(
        lower_kernel,
        out_shape=shape((leaves, nf, rank), BF16),
        in_specs=[SMEM, VMEM, HBM],
        out_specs=HBM,
        scratch_shapes=[
            pltpu.VMEM(down_shape, BF16),
            pltpu.VMEM((leaves, nf, rank), BF16),
            pltpu.VMEM((leaves, nf // 2, 2 * rank), F32),
            pltpu.VMEM((leaves, nf // 2, 2 * rank), F32),
            pltpu.VMEM((mids, nf // 2, 2 * rank), F32),
            pltpu.VMEM((mids, nf // 2, 2 * rank), F32),
            pltpu.SemaphoreType.DMA((mids + 1,)),
        ],
        compiler_params=pltpu.CompilerParams(vmem_limit_bytes=42000000),
        name="lower",
    )(slots, returned, down_all)
    return jnp.swapaxes(forward, 1, 2), jnp.swapaxes(adjoint, 1, 2)


def solution(mesh):
    placed = (
        P(("grp", "dev"), None, None),
        P(("grp", "dev"), None, None),
        P(("grp", "dev"), None, None),
        P(("grp", "dev"), None, None),
        P(("grp", "dev"), None, None, None),
        P(("grp", "dev"), None, None, None),
        P(("grp", "dev"), None, None, None),
        P(("grp", "dev"), None, None),
        P(("grp", "dev"), None),
        P(("grp", "dev"), None),
        P(("grp", "dev"), None),
    )
    return jax.shard_map(
        on_device,
        mesh=mesh,
        in_specs=placed,
        out_specs=(P(("grp", "dev"), None, None), P(("grp", "dev"), None, None)),
        check_vma=False,
    )
```
